256 devices in a mesh: fsdp: 16 (over x_lo, z), seq: 16 (over y, x_hi, core).
Axes of the slice: x: 4 (x_hi: 2, x_lo: 2; x = x_hi * 2 + x_lo), y: 4, z: 8, core: 2. Of those that a mesh axis runs over, the one named last changes fastest.
Arguments:
- normed_input: bfloat16 [16, 2048, 2048], P('fsdp', 'seq'), may hold values from -40 to 40
- out_grad: bfloat16 [16, 2048, 2048], P('fsdp', 'seq'), may hold values from -6 to 6
- w_query: bfloat16 [2048, 2048], P('fsdp', 'seq'), may hold values from -1 to 1
- key_weight_matrix: bfloat16 [2048, 512], P('fsdp'), may hold values from -1 to 1
- value_weight_matrix: bfloat16 [2048, 512], P('fsdp'), may hold values from -0.125 to 0.125
- boundary: int32 [16], P('fsdp'), may hold values from 1 to 2047
Outputs:
- input_grad: bfloat16 [16, 2048, 2048], P('fsdp', 'seq')
- grad_query_w: float32 [2048, 2048], P('fsdp', 'seq')
- grad_key_w: float32 [2048, 512], P('fsdp')
- grad_value_w: float32 [2048, 512], P('fsdp')
The draws below stay inside these ranges and needn't reach their ends.
All inputs are finite; a program needn't handle non-finite values.
Results may differ from the reference program's by a relative error of at most 0.034.
The reference program's roundings to bfloat16 on the way count: a program that leaves them out, or rounds other values in their place, can miss the bound.
Values may be sent and summed in bfloat16 or wider, within the bound.
A program may use at most 64 MiB of HBM per device.

```python
import jax
import jax.numpy as jnp
from jax import lax

MODEL_FEATURES = 2048
QUERY_HEADS = 16
KEY_VALUE_HEADS = 4
HEAD_SIZE = 128
SLICE_POSITIONS = 2048
BOOKS = 16
N_SEQ = 16


def query_normals(key):
    return jax.random.normal(jax.random.fold_in(key, 17), (MODEL_FEATURES, QUERY_HEADS * HEAD_SIZE), jnp.float32)


def draw_w_query(key, part):
    gaussian_draws = query_normals(key)
    return (jnp.clip(gaussian_draws, -6.0, 6.0) * MODEL_FEATURES ** (-0.5)).astype(jnp.bfloat16)


def draw_key_weight_matrix(key, part):
    key = jax.random.fold_in(key, 4)
    separate_terms = jax.random.normal(key, (MODEL_FEATURES, KEY_VALUE_HEADS * HEAD_SIZE), jnp.float32)
    mixed = separate_terms
    return (jnp.clip(mixed, -6.0, 6.0) * MODEL_FEATURES ** (-0.5)).astype(jnp.bfloat16)


def draw_normed_input(key, part):
    key = jax.random.fold_in(key, 5)
    key_base = jax.random.fold_in(key, 0)
    values = jnp.clip(jax.random.normal(key_base, (BOOKS, SLICE_POSITIONS, MODEL_FEATURES), jnp.float32), -6.0, 6.0)
    return values.astype(jnp.bfloat16)


def with_ends(values, rng, least, high):
    place = [jax.random.randint(jax.random.fold_in(rng, axis), (), 0, length) for axis, length in enumerate(values.shape)]
    longest = values.shape.index(max(values.shape))
    neighbour = place[:longest] + [(place[longest] + 1) % values.shape[longest]] + place[longest + 1:]
    return values.at[tuple(place)].set(least).at[tuple(neighbour)].set(high)


def shard_levels(rng, shape, pieces, low, high):
    def one(position, shards_of):
        heights = jax.random.uniform(jax.random.fold_in(jax.random.fold_in(rng, 6), position), (shards_of,), jnp.float32, low / len(pieces), high / len(pieces))
        return jnp.repeat(jnp.exp(heights), shape[position] // shards_of).reshape((-1,) + (1,) * (len(shape) - position - 1))

    factor_of = one(*pieces[0])
    for cut in pieces[1:]:
        factor_of = factor_of * one(*cut)
    return factor_of


def scatter_about(rng, extent, deviation, most, shards=(), kind=jnp.bfloat16):
    loudness = shard_levels(rng, extent, shards, -0.22, 0.18) if shards else 1.0
    drawn = jax.random.normal(rng, extent, jnp.float32) * deviation * loudness
    return jnp.minimum(jnp.maximum(drawn, -most), most).astype(kind)


def setup_inputs(seed: int = 0) -> dict:
    arg_keys = jax.random.split(jax.random.key(seed), 7)
    return {
        "normed_input": draw_normed_input(jax.random.fold_in(arg_keys[6], 71), 0),
        "out_grad": scatter_about(arg_keys[1], (BOOKS, SLICE_POSITIONS, QUERY_HEADS * HEAD_SIZE), 1.0, 6.0, ((0, 16), (1, 16))),
        "w_query": draw_w_query(jax.random.fold_in(arg_keys[6], 71), 0),
        "key_weight_matrix": draw_key_weight_matrix(jax.random.fold_in(arg_keys[6], 71), 0),
        "value_weight_matrix": scatter_about(arg_keys[4], (MODEL_FEATURES, KEY_VALUE_HEADS * HEAD_SIZE), MODEL_FEATURES ** -0.5, 0.125, ((0, 16),)),
        "boundary": with_ends(jax.random.randint(arg_keys[5], (BOOKS,), 1, SLICE_POSITIONS), jax.random.fold_in(arg_keys[5], 1), 1, SLICE_POSITIONS - 1).astype(jnp.int32),
    }


def rope_tables(length):
    half_size = HEAD_SIZE // 2
    inverse = 500000.0 ** (-(jnp.arange(half_size, dtype=jnp.float32) * 2.0 / HEAD_SIZE))
    angles = jnp.arange(length, dtype=jnp.float32)[:, None] * inverse[None, :]
    return jnp.cos(angles), jnp.sin(angles)


def apply_rotation(values, cosine_lookup, sine_lookup):
    half_size = values.shape[-1] // 2
    first_half = values[..., :half_size]
    second_half = values[..., half_size:]
    cosine_part = cosine_lookup[:, None, :]
    sine_part = sine_lookup[:, None, :]
    return jnp.concatenate([first_half * cosine_part - second_half * sine_part, second_half * cosine_part + first_half * sine_part], axis=-1)


def rounded_values(values):
    return lax.optimization_barrier(values.astype(jnp.bfloat16)).astype(jnp.float32)


def reference(normed_input, out_grad, w_query, key_weight_matrix, value_weight_matrix, boundary):
    group_count = QUERY_HEADS // KEY_VALUE_HEADS
    head_count = QUERY_HEADS // N_SEQ
    query_feature_width = QUERY_HEADS * HEAD_SIZE
    group_width = head_count * HEAD_SIZE
    score_scale = HEAD_SIZE ** -0.5
    cosine_lookup, sine_lookup = rope_tables(SLICE_POSITIONS)
    positions = jnp.arange(SLICE_POSITIONS, dtype=jnp.int32)
    key_expanded = jnp.repeat(key_weight_matrix.reshape(MODEL_FEATURES, KEY_VALUE_HEADS, HEAD_SIZE), group_count, axis=1).reshape(MODEL_FEATURES, query_feature_width)
    value_expanded = jnp.repeat(value_weight_matrix.reshape(MODEL_FEATURES, KEY_VALUE_HEADS, HEAD_SIZE), group_count, axis=1).reshape(MODEL_FEATURES, query_feature_width)
    wide_weights = jnp.concatenate([w_query, key_expanded, value_expanded], axis=1).astype(jnp.float32)
    group_weights = jnp.transpose(wide_weights.reshape(MODEL_FEATURES, 3, N_SEQ, group_width), (2, 0, 1, 3)).reshape(N_SEQ, MODEL_FEATURES, 3 * group_width)

    def one_book(running_total, inputs):
        volume_rows, grad_flat, book_start = inputs
        queries = rounded_values(apply_rotation(jnp.dot(volume_rows, w_query, preferred_element_type=jnp.float32).reshape(SLICE_POSITIONS, QUERY_HEADS, HEAD_SIZE), cosine_lookup, sine_lookup))
        key_head_rows = rounded_values(apply_rotation(jnp.dot(volume_rows, key_weight_matrix, preferred_element_type=jnp.float32).reshape(SLICE_POSITIONS, KEY_VALUE_HEADS, HEAD_SIZE), cosine_lookup, sine_lookup))
        value_head_rows = rounded_values(jnp.dot(volume_rows, value_weight_matrix, preferred_element_type=jnp.float32)).reshape(SLICE_POSITIONS, KEY_VALUE_HEADS, HEAD_SIZE)
        key_by_head = jnp.transpose(jnp.repeat(key_head_rows, group_count, axis=1), (1, 0, 2))
        value_by_head = jnp.transpose(jnp.repeat(value_head_rows, group_count, axis=1), (1, 0, 2))
        query_by_head = jnp.transpose(queries, (1, 0, 2))
        grad_by_head = jnp.transpose(grad_flat.astype(jnp.float32).reshape(SLICE_POSITIONS, QUERY_HEADS, HEAD_SIZE), (1, 0, 2))
        query_pos = positions[:, None]
        key_pos = positions[None, :]
        allowed = (key_pos <= query_pos) & ((query_pos < book_start) == (key_pos < book_start))

        def one_head(head_inputs):
            query_h, key_h, value_h, grad_h = head_inputs
            scores = jnp.dot(query_h, key_h.T, preferred_element_type=jnp.float32) * score_scale
            scores = jnp.where(allowed, scores, -1e30)
            row_max = jnp.max(scores, axis=-1, keepdims=True)
            exponent = jnp.exp(scores - row_max)
            prob_full = exponent / jnp.sum(exponent, axis=-1, keepdims=True)
            prob_low = rounded_values(prob_full)
            context = jnp.dot(prob_low, value_h, preferred_element_type=jnp.float32)
            row_delta = jnp.sum(grad_h * context, axis=-1)
            prob_grad = jnp.dot(grad_h, value_h.T, preferred_element_type=jnp.float32)
            score_grad = rounded_values(prob_full * (prob_grad - row_delta[:, None]))
            query_grad_h = jnp.dot(score_grad, key_h, preferred_element_type=jnp.float32) * score_scale
            key_grad_h = jnp.dot(score_grad.T, query_h, preferred_element_type=jnp.float32) * score_scale
            value_grad_h = jnp.dot(prob_low.T, grad_h, preferred_element_type=jnp.float32)
            return query_grad_h, key_grad_h, value_grad_h

        query_grad, key_grad, value_grad = lax.map(one_head, (query_by_head, key_by_head, value_by_head, grad_by_head))
        query_grad = apply_rotation(jnp.transpose(query_grad, (1, 0, 2)), cosine_lookup, -sine_lookup).astype(jnp.bfloat16)
        key_grad = apply_rotation(jnp.transpose(key_grad, (1, 0, 2)), cosine_lookup, -sine_lookup).astype(jnp.bfloat16)
        value_grad = jnp.transpose(value_grad, (1, 0, 2)).astype(jnp.bfloat16)
        grad_cols = jnp.concatenate([query_grad.reshape(SLICE_POSITIONS, query_feature_width), key_grad.reshape(SLICE_POSITIONS, query_feature_width), value_grad.reshape(SLICE_POSITIONS, query_feature_width)], axis=1)
        weight_gradient = jnp.dot(volume_rows.T, grad_cols, preferred_element_type=jnp.float32)
        query_sum = running_total[0] + weight_gradient[:, :query_feature_width]
        key_total_sum = running_total[1] + weight_gradient[:, query_feature_width:2 * query_feature_width].reshape(MODEL_FEATURES, KEY_VALUE_HEADS, group_count, HEAD_SIZE).sum(axis=2).reshape(MODEL_FEATURES, KEY_VALUE_HEADS * HEAD_SIZE)
        value_total_sum = running_total[2] + weight_gradient[:, 2 * query_feature_width:].reshape(MODEL_FEATURES, KEY_VALUE_HEADS, group_count, HEAD_SIZE).sum(axis=2).reshape(MODEL_FEATURES, KEY_VALUE_HEADS * HEAD_SIZE)
        group_cols = jnp.transpose(grad_cols.astype(jnp.float32).reshape(SLICE_POSITIONS, 3, N_SEQ, group_width), (2, 0, 1, 3)).reshape(N_SEQ, SLICE_POSITIONS, 3 * group_width)

        def add_group(input_total, group_inputs):
            cols_j, weights_j = group_inputs
            partial_j = jnp.dot(cols_j, weights_j.T, preferred_element_type=jnp.float32)
            return input_total + rounded_values(partial_j), None

        input_total, unused = lax.scan(add_group, jnp.zeros((SLICE_POSITIONS, MODEL_FEATURES), jnp.float32), (group_cols, group_weights))
        return (query_sum, key_total_sum, value_total_sum), input_total.astype(jnp.bfloat16)

    starting_state = (jnp.zeros((MODEL_FEATURES, query_feature_width), jnp.float32), jnp.zeros((MODEL_FEATURES, KEY_VALUE_HEADS * HEAD_SIZE), jnp.float32), jnp.zeros((MODEL_FEATURES, KEY_VALUE_HEADS * HEAD_SIZE), jnp.float32))
    totals, input_grad = lax.scan(one_book, starting_state, (normed_input, out_grad, boundary))
    return input_grad, totals[0], totals[1], totals[2]
```

```python
import functools

import jax
import jax.numpy as jnp
import numpy as np
from jax import lax
from jax.experimental import pallas as pl
from jax.experimental.pallas import tpu as pltpu
from jax.sharding import PartitionSpec as P

HEAD = 128
N_SEQ = 16
N_FSDP = 16
ROWS = 128
LENGTH = 2048
FEATURES = 2048
GROUP = 4
MESH = pl.DeviceIdType.MESH
SCALE = HEAD ** (-0.5)
EXP2_SCALE = SCALE * 1.4426950408889634

GATHER = (
    ("up", (0, 0), 0, 64, (-1, 0)),
    ("down", (0, 0), 64, 64, (1, 0)),
    ("side", (0, 0), 0, 64, (0, 1)),
    ("up", (0, 0), 64, 64, (-1, 0)),
    ("down", (0, 0), 0, 64, (1, 0)),
    ("side", (0, 0), 64, 64, (0, 1)),
    ("up", (-1, 0), 0, 64, (2, 0)),
    ("down", (1, 0), 64, 64, (2, 0)),
    ("side", (-1, 0), 0, 64, (-1, 1)),
    ("side", (1, 0), 64, 64, (1, 1)),
    ("down", (0, 1), 0, 64, (1, 1)),
    ("up", (0, 1), 64, 64, (-1, 1)),
    ("up", (-1, 1), 0, 48, (2, 1)),
    ("down", (1, 1), 80, 48, (2, 1)),
    ("side", (2, 0), 48, 32, (2, 1)),
)

REDUCE = (
    ("down", (2, 1), 0, 48, (-1, 1)),
    ("up", (2, 1), 80, 48, (1, 1)),
    ("side", (2, 1), 48, 32, (2, 0)),
    ("side", (-1, 1), 0, 64, (-1, 0)),
    ("side", (1, 1), 64, 64, (1, 0)),
    ("down", (-1, 1), 64, 64, (0, 1)),
    ("up", (1, 1), 0, 64, (0, 1)),
    ("down", (2, 0), 0, 64, (-1, 0)),
    ("up", (2, 0), 64, 64, (1, 0)),
    ("side", (0, 1), 0, 128, (0, 0)),
    ("down", (-1, 0), 0, 128, (0, 0)),
    ("up", (1, 0), 0, 128, (0, 0)),
)


class Place:
    def __init__(self):
        self.f = lax.axis_index("fsdp")
        self.s = lax.axis_index("seq")
        self.core = lax.rem(self.s, 2)
        self.hi = lax.rem(lax.div(self.s, 2), 2)
        self.y = lax.div(self.s, 4)
        self.z = lax.rem(self.f, 8)
        self.lo = lax.div(self.f, 8)

    def to(self, direction):
        s = self.s
        if direction == "up":
            return (self.f, lax.rem(s + 4, N_SEQ))
        if direction == "down":
            return (self.f, lax.rem(s + 12, N_SEQ))
        if direction == "side":
            return (self.f, s + 2 - 4 * self.hi)
        return (self.f, s + 1 - 2 * self.core)

    def block(self, rel, other_core=0):
        dy, dh = rel
        y = lax.rem(self.y + dy + 4, 4)
        hi = 1 - self.hi if dh else self.hi
        core = 1 - self.core if other_core else self.core
        return y * 4 + hi * 2 + core


def enter(place, fsdp_peers):
    barrier = pltpu.get_barrier_semaphore()

    def greet(j, carry):
        pl.semaphore_signal(
            barrier,
            inc=1,
            device_id=(place.f, lax.rem(place.s + j, N_SEQ)),
            device_id_type=MESH,
        )
        pl.semaphore_signal(
            barrier,
            inc=1,
            device_id=(lax.rem(place.f + j, N_FSDP), place.s),
            device_id_type=MESH,
        )
        return carry

    lax.fori_loop(1, N_SEQ, greet, 0)
    pl.semaphore_wait(barrier, 2 * (N_SEQ - 1))


def remote(src, dst, send, recv, device):
    return pltpu.make_async_remote_copy(
        src_ref=src,
        dst_ref=dst,
        send_sem=send,
        recv_sem=recv,
        device_id=device,
        device_id_type=MESH,
    )


def gather_kernel(
    x_ref, g_ref, wq_ref, wk_ref, wv_ref, cos_ref, sin_ref,
    rows_out, q_ref, k_ref, v_ref, grad_ref, w_ref,
    rows, kv, x_send, x_recv, c_send, c_recv, g_send, g_recv, w_send, w_recv, o_sem,
):
    me = Place()
    own = pl.multiple_of(me.s * ROWS, ROWS)
    w_own = pl.multiple_of(me.f * ROWS, ROWS)
    kv_col = pl.multiple_of(HEAD + me.core * HEAD, HEAD)
    kv_other = pl.multiple_of(HEAD + (1 - me.core) * HEAD, HEAD)
    head_col = pl.multiple_of(me.y * HEAD, HEAD)
    kv[...] = jnp.where(
        me.core == 0,
        wk_ref[:, pl.ds(head_col, HEAD)].astype(jnp.float32),
        wv_ref[:, pl.ds(head_col, HEAD)].astype(jnp.float32),
    ).astype(jnp.bfloat16)
    w_ref[pl.ds(w_own, ROWS), :HEAD] = wq_ref[...]
    w_ref[pl.ds(w_own, ROWS), pl.ds(kv_col, HEAD)] = kv[...]
    rows[pl.ds(own, ROWS), :] = x_ref[...]
    grad_ref[pl.ds(own, ROWS), :] = g_ref[:, pl.ds(own, HEAD)]
    enter(me, True)

    def w_copies(j, device_f, source_f):
        at = pl.multiple_of(source_f * ROWS, ROWS)
        device = (device_f, me.s)
        return (
            remote(wq_ref, w_ref.at[pl.ds(at, ROWS), :HEAD], w_send.at[0, j], w_recv.at[0, j], device),
            remote(kv, w_ref.at[pl.ds(at, ROWS), pl.ds(kv_col, HEAD)], w_send.at[1, j], w_recv.at[1, j], device),
        )

    def w_start(j, carry):
        for copy in w_copies(j, lax.rem(me.f + j, N_FSDP), me.f):
            copy.start()
        return carry

    def part(rel, first, count, other_core=0):
        at = pl.multiple_of(me.block(rel, other_core) * ROWS + first, 16)
        return rows.at[pl.ds(at, count), :]

    def x_start(i):
        direction, rel, first, count, _ = GATHER[i]
        piece = part(rel, first, count)
        remote(piece, piece, x_send.at[i], x_recv.at[i], me.to(direction)).start()

    def x_arrived(i):
        direction, _, first, count, rel = GATHER[i]
        piece = part(rel, first, count)
        remote(piece, piece, x_send.at[i], x_recv.at[i], me.to(direction)).wait_recv()
        core_copy(i).start()

    def core_piece(i):
        if i == len(GATHER):
            return (0, 0), 0, 128
        _, _, first, count, rel = GATHER[i]
        return rel, first, count

    def core_copy(i, receive=False):
        piece = part(*core_piece(i), other_core=1 if receive else 0)
        return remote(piece, piece, c_send.at[i], c_recv.at[i], me.to("core"))

    def g_copy(j, device_s, source_s):
        at = pl.multiple_of(source_s * ROWS, ROWS)
        col = pl.multiple_of(device_s * HEAD, HEAD)
        return remote(
            g_ref.at[:, pl.ds(col, HEAD)],
            grad_ref.at[pl.ds(at, ROWS), :],
            g_send.at[j],
            g_recv.at[j],
            (me.f, device_s),
        )

    def g_start(j, carry):
        g_copy(j, lax.rem(me.s + j, N_SEQ), me.s).start()
        return carry

    for i in range(6):
        x_start(i)
    lax.fori_loop(1, N_FSDP, w_start, 0)
    core_copy(len(GATHER)).start()
    x_arrived(0)
    x_start(6)
    x_start(8)
    x_arrived(1)
    x_start(7)
    x_start(9)
    x_arrived(2)
    x_start(10)
    x_arrived(5)
    x_start(11)
    x_arrived(3)
    x_arrived(4)
    lax.fori_loop(1, N_SEQ, g_start, 0)
    x_arrived(8)
    x_start(12)
    x_arrived(9)
    x_start(13)
    x_arrived(6)
    x_arrived(7)
    x_start(14)

    def w_finish(j, carry):
        for copy in w_copies(j, lax.rem(me.f + N_FSDP - j, N_FSDP), lax.rem(me.f + N_FSDP - j, N_FSDP)):
            copy.wait_recv()
        for copy in w_copies(j, lax.rem(me.f + j, N_FSDP), me.f):
            copy.wait_send()
        return carry

    lax.fori_loop(1, N_FSDP, w_finish, 0)
    mine = w_ref.at[:, pl.ds(kv_col, HEAD)]
    theirs = w_ref.at[:, pl.ds(kv_other, HEAD)]
    share = remote(mine, mine, w_send.at[0, 0], w_recv.at[0, 0], me.to("core"))
    share.start()
    x_arrived(10)
    x_arrived(11)
    x_arrived(12)
    x_arrived(13)
    x_arrived(14)
    share.wait_send()
    remote(theirs, theirs, w_send.at[0, 0], w_recv.at[0, 0], me.to("core")).wait_recv()
    for i in range(len(GATHER) + 1):
        core_copy(i, True).wait_recv()
    save = pltpu.make_async_copy(rows, rows_out, o_sem.at[0])
    save.start()

    def project(c, carry):
        at = pl.ds(pl.multiple_of(c * 256, 256), 256)
        full = jnp.dot(rows[at, :], w_ref[...], preferred_element_type=jnp.float32)
        cos, sin = cos_ref[at, :], sin_ref[at, :]
        q, k = full[:, :HEAD], full[:, HEAD : 2 * HEAD]
        q_ref[at, :] = (q * cos + pltpu.roll(q, HEAD // 2, 1) * sin).astype(jnp.bfloat16)
        k_ref[at, :] = (k * cos + pltpu.roll(k, HEAD // 2, 1) * sin).astype(jnp.bfloat16)
        v_ref[at, :] = full[:, 2 * HEAD :].astype(jnp.bfloat16)
        return carry

    lax.fori_loop(0, LENGTH // 256, project, 0)

    def g_finish(j, carry):
        back = lax.rem(me.s + N_SEQ - j, N_SEQ)
        g_copy(j, back, back).wait_recv()
        g_copy(j, lax.rem(me.s + j, N_SEQ), me.s).wait_send()
        return carry

    lax.fori_loop(1, N_SEQ, g_finish, 0)
    for i in range(len(GATHER)):
        direction, rel, first, count, _ = GATHER[i]
        piece = part(rel, first, count)
        remote(piece, piece, x_send.at[i], x_recv.at[i], me.to(direction)).wait_send()
    for i in range(len(GATHER) + 1):
        core_copy(i).wait_send()
    save.wait()


NT = (((1,), (1,)), ((), ()))
TN = (((0,), (0,)), ((), ()))
QB = 256


def attention_kernel(b_ref, q_ref, k_ref, v_ref, g_ref, cos_ref, sin_ref, out_ref, sc, dp_sc, dk_sc, dv_sc, kt_sc):
    start = b_ref[0]
    kt_sc[...] = k_ref[...].T
    for i in range(LENGTH // QB):
        rows_i = pl.ds(i * QB, QB)
        q = q_ref[rows_i, :]
        g = g_ref[rows_i, :]
        q_pos = i * QB + lax.broadcasted_iota(jnp.int32, (1, QB), 1)
        low = jnp.where(q_pos < start, 0, start)
        top = jnp.full((1, QB), -1e30, jnp.float32)
        for j in range(i + 1):
            at = pl.ds(j * QB, QB)
            s = lax.dot_general(k_ref[at, :], q, NT, preferred_element_type=jnp.float32)
            k_pos = j * QB + lax.broadcasted_iota(jnp.int32, (QB, QB), 0)
            ok = k_pos >= low
            if j == i:
                ok = ok & (k_pos <= q_pos)
            s = jnp.where(ok, s, -1e30)
            sc[at, :] = s
            top = jnp.maximum(top, jnp.max(s, axis=0, keepdims=True))
        top = top * EXP2_SCALE
        total = jnp.zeros((1, QB), jnp.float32)
        for j in range(i + 1):
            at = pl.ds(j * QB, QB)
            e = jnp.exp2(sc[at, :] * EXP2_SCALE - top)
            sc[at, :] = e
            total = total + jnp.sum(e, axis=0, keepdims=True)
        inverse = 1.0 / total
        delta = jnp.zeros((1, QB), jnp.float32)
        for j in range(i + 1):
            at = pl.ds(j * QB, QB)
            p = sc[at, :] * inverse
            sc[at, :] = p
            low_p = p.astype(jnp.bfloat16)
            d = lax.dot_general(v_ref[at, :], g, NT, preferred_element_type=jnp.float32)
            dp_sc[at, :] = d
            delta = delta + jnp.sum(low_p.astype(jnp.float32) * d, axis=0, keepdims=True)
            dv = jnp.dot(low_p, g, preferred_element_type=jnp.float32)
            if j == i:
                dv_sc[at, :] = dv
            else:
                dv_sc[at, :] += dv
        dq = jnp.zeros((HEAD, QB), jnp.float32)
        for j in range(i + 1):
            at = pl.ds(j * QB, QB)
            ds = (sc[at, :] * (dp_sc[at, :] - delta)).astype(jnp.bfloat16)
            dk = jnp.dot(ds, q, preferred_element_type=jnp.float32)
            if j == i:
                dk_sc[at, :] = dk
            else:
                dk_sc[at, :] += dk
            dq = dq + jnp.dot(kt_sc[:, at], ds, preferred_element_type=jnp.float32)
        dq = dq.T * SCALE
        out_ref[rows_i, :HEAD] = (
            dq * cos_ref[rows_i, :] - pltpu.roll(dq, HEAD // 2, 1) * sin_ref[rows_i, :]
        ).astype(jnp.bfloat16)

    def finish(c, carry):
        at = pl.ds(pl.multiple_of(c * QB, QB), QB)
        dk = dk_sc[at, :] * SCALE
        out_ref[at, HEAD : 2 * HEAD] = (
            dk * cos_ref[at, :] - pltpu.roll(dk, HEAD // 2, 1) * sin_ref[at, :]
        ).astype(jnp.bfloat16)
        out_ref[at, 2 * HEAD :] = dv_sc[at, :].astype(jnp.bfloat16)
        return carry

    lax.fori_loop(0, LENGTH // QB, finish, 0)


ORDER = ((2, 1), (-1, 1), (1, 1), (2, 0), (0, 1), (-1, 0), (1, 0), (0, 0))
SLOT = {rel: n for n, rel in enumerate(ORDER)}
RECV_AT = []
_at = 0
for _piece in REDUCE:
    RECV_AT.append(_at)
    _at += _piece[3]
RECV_ROWS = _at


def scatter_kernel(
    g_ref, w_ref, rows_hbm,
    in_ref, dq_ref, dk_ref, dv_ref,
    rows, mine, away, near, arrived, dwt, kv_near, lo_in, z_in, kv_all,
    r_send, r_recv, n_send, n_recv, kv_sem, lo_sem, z_send, z_recv, a_send, a_recv, l_sem,
):
    me = Place()
    load = pltpu.make_async_copy(rows_hbm, rows, l_sem.at[0])
    load.start()
    enter(me, True)

    def partial_sum(rel, other_core):
        at = pl.ds(pl.multiple_of(me.block(rel, other_core) * ROWS, ROWS), ROWS)
        return lax.dot_general(
            g_ref[at, :], w_ref[...], NT, preferred_element_type=jnp.float32
        ).astype(jnp.bfloat16)

    def near_copy(n):
        return remote(away.at[n], near.at[n], n_send.at[n], n_recv.at[n], me.to("core"))

    def block_out(rel):
        n = SLOT[rel]
        away[n] = partial_sum(rel, 1)
        near_copy(n).start()
        mine[n] = partial_sum(rel, 0)

    def block_in(rel):
        n = SLOT[rel]
        near_copy(n).wait_recv()
        mine[n] = (mine[n].astype(jnp.float32) + near[n].astype(jnp.float32)).astype(jnp.bfloat16)

    def r_copy(i):
        direction, rel, first, count, _ = REDUCE[i]
        return remote(
            mine.at[SLOT[rel], pl.ds(first, count), :],
            arrived.at[pl.ds(RECV_AT[i], count), :],
            r_send.at[i],
            r_recv.at[i],
            me.to(direction),
        )

    def r_add(i):
        _, _, first, count, rel = REDUCE[i]
        r_copy(i).wait_recv()
        n = SLOT[rel]
        mine[n, pl.ds(first, count), :] = (
            mine[n, pl.ds(first, count), :].astype(jnp.float32)
            + arrived[pl.ds(RECV_AT[i], count), :].astype(jnp.float32)
        ).astype(jnp.bfloat16)

    block_out((2, 1))
    block_out((-1, 1))
    block_in((2, 1))
    for i in (0, 1, 2):
        r_copy(i).start()
    load.wait()

    kv_row = pl.multiple_of(HEAD + me.core * HEAD, HEAD)
    kv_other = pl.multiple_of(HEAD + (1 - me.core) * HEAD, HEAD)
    q_rows = pl.ds(0, HEAD)

    def weights(c, carry):
        at = pl.ds(pl.multiple_of(c * 512, 512), 512)
        dwt[:, at] = lax.dot_general(
            g_ref[...], rows[:, at], TN, preferred_element_type=jnp.float32
        ).astype(jnp.bfloat16)
        return carry

    lax.fori_loop(0, FEATURES // 512, weights, 0)
    kv_copy = remote(dwt.at[pl.ds(kv_other, HEAD), :], kv_near, kv_sem.at[0], kv_sem.at[1], me.to("core"))
    kv_copy.start()
    block_out((1, 1))
    block_out((2, 0))
    kv_copy.wait_recv()
    kv_rows = pl.ds(kv_row, HEAD)
    dwt[kv_rows, :] = (
        dwt[kv_rows, :].astype(jnp.float32) + kv_near[...].astype(jnp.float32)
    ).astype(jnp.bfloat16)

    half = N_FSDP // 2 * ROWS
    away_cols = pl.ds(pl.multiple_of((1 - me.lo) * half, half), half)
    own_cols = pl.ds(pl.multiple_of(me.lo * half, half), half)
    lo_device = ((1 - me.lo) * 8 + me.z, me.s)
    lo_q = remote(dwt.at[q_rows, away_cols], lo_in.at[0], lo_sem.at[0], lo_sem.at[1], lo_device)
    lo_kv = remote(dwt.at[kv_rows, away_cols], lo_in.at[1], lo_sem.at[2], lo_sem.at[3], lo_device)
    lo_q.start()
    lo_kv.start()

    block_in((-1, 1))
    r_add(0)
    r_copy(3).start()
    r_copy(5).start()
    block_in((1, 1))
    r_add(1)
    r_copy(4).start()
    r_copy(6).start()
    block_in((2, 0))
    r_add(2)
    r_copy(7).start()
    r_copy(8).start()
    block_out((0, 1))
    block_out((-1, 0))
    block_out((1, 0))
    block_out((0, 0))

    lo_q.wait_recv()
    lo_kv.wait_recv()
    lo_q.wait_send()
    lo_kv.wait_send()
    dwt[q_rows, own_cols] = (
        dwt[q_rows, own_cols].astype(jnp.float32) + lo_in[0].astype(jnp.float32)
    ).astype(jnp.bfloat16)
    dwt[kv_rows, own_cols] = (
        dwt[kv_rows, own_cols].astype(jnp.float32) + lo_in[1].astype(jnp.float32)
    ).astype(jnp.bfloat16)

    def z_copies(j, z_to):
        cols = pl.ds(pl.multiple_of((me.lo * 8 + z_to) * ROWS, ROWS), ROWS)
        device = (me.lo * 8 + z_to, me.s)
        return (
            remote(dwt.at[q_rows, cols], z_in.at[j, 0], z_send.at[0, j], z_recv.at[0, j], device),
            remote(dwt.at[kv_rows, cols], z_in.at[j, 1], z_send.at[1, j], z_recv.at[1, j], device),
        )

    def z_start(j, carry):
        for copy in z_copies(j, lax.rem(me.z + j, 8)):
            copy.start()
        return carry

    lax.fori_loop(1, 8, z_start, 0)

    block_in((0, 1))
    r_add(5)
    r_add(6)
    r_copy(9).start()
    block_in((-1, 0))
    r_add(3)
    r_add(7)
    r_copy(10).start()
    block_in((1, 0))
    r_add(4)
    r_add(8)
    r_copy(11).start()
    block_in((0, 0))

    own_piece = pl.ds(pl.multiple_of(me.f * ROWS, ROWS), ROWS)

    def z_add(j, sums):
        for copy in z_copies(j, lax.rem(me.z + j, 8)):
            copy.wait()
        return sums[0] + z_in[j, 0].astype(jnp.float32), sums[1] + z_in[j, 1].astype(jnp.float32)

    q_sum, kv_sum = lax.fori_loop(
        1,
        8,
        z_add,
        (dwt[q_rows, own_piece].astype(jnp.float32), dwt[kv_rows, own_piece].astype(jnp.float32)),
    )
    own_slot = kv_all.at[me.s]
    own_slot[...] = kv_sum.astype(jnp.bfloat16)

    def a_copy(j, source):
        return remote(
            kv_all.at[source],
            kv_all.at[source],
            a_send.at[j],
            a_recv.at[j],
            (me.f, lax.rem(me.s + j, N_SEQ)),
        )

    def a_start(j, carry):
        a_copy(j, me.s).start()
        return carry

    lax.fori_loop(1, N_SEQ, a_start, 0)
    dq_ref[...] = q_sum.T

    r_copy(9).wait_recv()
    r_copy(10).wait_recv()
    r_copy(11).wait_recv()
    n = SLOT[(0, 0)]
    total = mine[n].astype(jnp.float32)
    for i in (9, 10, 11):
        total = total + arrived[pl.ds(RECV_AT[i], ROWS), :].astype(jnp.float32)
    in_ref[...] = total.astype(jnp.bfloat16)

    def a_finish(j, carry):
        a_copy(j, lax.rem(me.s + N_SEQ - j, N_SEQ)).wait_recv()
        a_copy(j, me.s).wait_send()
        return carry

    lax.fori_loop(1, N_SEQ, a_finish, 0)
    for g in range(4):
        at = pl.ds(g * HEAD, HEAD)
        dk_ref[:, at] = (kv_all[4 * g].astype(jnp.float32) + kv_all[4 * g + 2].astype(jnp.float32)).T
        dv_ref[:, at] = (kv_all[4 * g + 1].astype(jnp.float32) + kv_all[4 * g + 3].astype(jnp.float32)).T

    kv_copy.wait_send()
    for i in range(len(REDUCE)):
        r_copy(i).wait_send()
    for n in range(len(ORDER)):
        near_copy(n).wait_send()


def rope_tables():
    half = HEAD // 2
    inverse = (500000.0 ** (-(np.arange(half, dtype=np.float64) * 2.0 / HEAD))).astype(np.float32)
    angles = np.arange(LENGTH, dtype=np.float32)[:, None] * inverse[None, :]
    cos, sin = np.cos(angles), np.sin(angles)
    return np.concatenate([cos, cos], axis=1), np.concatenate([-sin, sin], axis=1)


def vmem():
    return pl.BlockSpec(memory_space=pltpu.VMEM)


def shards(normed_input, out_grad, w_query, key_weight_matrix, value_weight_matrix, boundary):
    cos, sin = rope_tables()
    cos, sin = jnp.asarray(cos), jnp.asarray(sin)
    bf16, f32 = jnp.bfloat16, jnp.float32
    dma = pltpu.SemaphoreType.DMA
    shape = jax.ShapeDtypeStruct
    per_head = shape((LENGTH, HEAD), bf16)
    rows, q, k, v, g, w = pl.pallas_call(
        gather_kernel,
        out_shape=(shape((LENGTH, FEATURES), bf16), per_head, per_head, per_head, per_head, shape((FEATURES, 3 * HEAD), bf16)),
        in_specs=[vmem()] * 7,
        out_specs=(pl.BlockSpec(memory_space=pl.ANY),) + (vmem(),) * 5,
        scratch_shapes=[
            pltpu.VMEM((LENGTH, FEATURES), bf16),
            pltpu.VMEM((ROWS, HEAD), bf16),
            dma((len(GATHER),)),
            dma((len(GATHER),)),
            dma((len(GATHER) + 1,)),
            dma((len(GATHER) + 1,)),
            dma((N_SEQ,)),
            dma((N_SEQ,)),
            dma((2, N_FSDP)),
            dma((2, N_FSDP)),
            dma((1,)),
        ],
        compiler_params=pltpu.CompilerParams(collective_id=1, has_side_effects=True, vmem_limit_bytes=40 * 2**20),
        name="gather_project",
    )(normed_input[0], out_grad[0], w_query, key_weight_matrix, value_weight_matrix, cos, sin)

    grads = pl.pallas_call(
        attention_kernel,
        out_shape=shape((LENGTH, 3 * HEAD), bf16),
        in_specs=[pl.BlockSpec(memory_space=pltpu.SMEM)] + [vmem()] * 6,
        out_specs=vmem(),
        scratch_shapes=[
            pltpu.VMEM((LENGTH, QB), f32),
            pltpu.VMEM((LENGTH, QB), f32),
            pltpu.VMEM((LENGTH, HEAD), f32),
            pltpu.VMEM((LENGTH, HEAD), f32),
            pltpu.VMEM((HEAD, LENGTH), bf16),
        ],
        compiler_params=pltpu.CompilerParams(vmem_limit_bytes=40 * 2**20),
        name="attention_grads",
    )(boundary, q, k, v, g, cos, sin)

    input_grad, dq, dk, dv = pl.pallas_call(
        scatter_kernel,
        out_shape=(
            shape((ROWS, FEATURES), bf16),
            shape((ROWS, HEAD), f32),
            shape((ROWS, GROUP * HEAD), f32),
            shape((ROWS, GROUP * HEAD), f32),
        ),
        in_specs=[vmem(), vmem(), pl.BlockSpec(memory_space=pl.ANY)],
        out_specs=(vmem(),) * 4,
        scratch_shapes=[
            pltpu.VMEM((LENGTH, FEATURES), bf16),
            pltpu.VMEM((8, ROWS, FEATURES), bf16),
            pltpu.VMEM((8, ROWS, FEATURES), bf16),
            pltpu.VMEM((8, ROWS, FEATURES), bf16),
            pltpu.VMEM((RECV_ROWS, FEATURES), bf16),
            pltpu.VMEM((3 * HEAD, FEATURES), bf16),
            pltpu.VMEM((HEAD, FEATURES), bf16),
            pltpu.VMEM((2, HEAD, FEATURES // 2), bf16),
            pltpu.VMEM((8, 2, HEAD, ROWS), bf16),
            pltpu.VMEM((N_SEQ, HEAD, ROWS), bf16),
            dma((len(REDUCE),)),
            dma((len(REDUCE),)),
            dma((len(ORDER),)),
            dma((len(ORDER),)),
            dma((2,)),
            dma((4,)),
            dma((2, 8)),
            dma((2, 8)),
            dma((N_SEQ,)),
            dma((N_SEQ,)),
            dma((1,)),
        ],
        compiler_params=pltpu.CompilerParams(collective_id=2, has_side_effects=True, vmem_limit_bytes=48 * 2**20),
        name="scatter_grads",
    )(grads, w, rows)
    return (input_grad[None], dq, dk, dv)


def solution(mesh):
    return jax.shard_map(
        shards,
        mesh=mesh,
        in_specs=(
            P("fsdp", "seq", None),
            P("fsdp", "seq", None),
            P("fsdp", "seq"),
            P("fsdp", None),
            P("fsdp", None),
            P("fsdp"),
        ),
        out_specs=(P("fsdp", "seq", None), P("fsdp", "seq"), P("fsdp", None), P("fsdp", None)),
        check_vma=False,
    )
```

```python
import jax
import jax.numpy as jnp
import numpy as np
from jax import lax
from jax.experimental import pallas as pl
from jax.experimental.pallas import tpu as pltpu
from jax.sharding import PartitionSpec as P

HEAD = 128
N_SEQ = 16
N_FSDP = 16
ROWS = 128
LENGTH = 2048
FEATURES = 2048
GROUP = 4
MESH = pl.DeviceIdType.MESH
SCALE = HEAD ** (-0.5)
EXP2_SCALE = SCALE * 1.4426950408889634

GATHER = (
    ("up", (0, 0), 0, 64, (-1, 0)),
    ("down", (0, 0), 64, 64, (1, 0)),
    ("side", (0, 0), 0, 64, (0, 1)),
    ("up", (0, 0), 64, 64, (-1, 0)),
    ("down", (0, 0), 0, 64, (1, 0)),
    ("side", (0, 0), 64, 64, (0, 1)),
    ("up", (-1, 0), 0, 64, (2, 0)),
    ("down", (1, 0), 64, 64, (2, 0)),
    ("side", (-1, 0), 0, 64, (-1, 1)),
    ("side", (1, 0), 64, 64, (1, 1)),
    ("down", (0, 1), 0, 64, (1, 1)),
    ("up", (0, 1), 64, 64, (-1, 1)),
    ("up", (-1, 1), 0, 48, (2, 1)),
    ("down", (1, 1), 80, 48, (2, 1)),
    ("side", (2, 0), 48, 32, (2, 1)),
)

REDUCE = (
    ("down", (2, 1), 0, 48, (-1, 1)),
    ("up", (2, 1), 80, 48, (1, 1)),
    ("side", (2, 1), 48, 32, (2, 0)),
    ("down", (-1, 1), 64, 64, (0, 1)),
    ("up", (1, 1), 0, 64, (0, 1)),
    ("side", (-1, 1), 0, 64, (-1, 0)),
    ("side", (1, 1), 64, 64, (1, 0)),
    ("down", (2, 0), 0, 64, (-1, 0)),
    ("up", (2, 0), 64, 64, (1, 0)),
    ("down", (-1, 0), 64, 64, (0, 0)),
    ("up", (1, 0), 0, 64, (0, 0)),
    ("side", (0, 1), 0, 64, (0, 0)),
    ("side", (0, 1), 64, 64, (0, 0)),
    ("down", (-1, 0), 0, 64, (0, 0)),
    ("up", (1, 0), 64, 64, (0, 0)),
)
LAST = ((0, (10, 11, 13)), (64, (9, 12, 14)))


class Place:
    def __init__(self):
        self.f = lax.axis_index("fsdp")
        self.s = lax.axis_index("seq")
        self.core = lax.rem(self.s, 2)
        self.hi = lax.rem(lax.div(self.s, 2), 2)
        self.y = lax.div(self.s, 4)
        self.z = lax.rem(self.f, 8)
        self.lo = lax.div(self.f, 8)

    def to(self, direction):
        s = self.s
        if direction == "up":
            return (self.f, lax.rem(s + 4, N_SEQ))
        if direction == "down":
            return (self.f, lax.rem(s + 12, N_SEQ))
        if direction == "side":
            return (self.f, s + 2 - 4 * self.hi)
        if direction == "lo":
            return ((1 - self.lo) * 8 + self.z, s)
        return (self.f, s + 1 - 2 * self.core)

    def block(self, rel, other_core=0):
        dy, dh = rel
        y = lax.rem(self.y + dy + 4, 4)
        hi = 1 - self.hi if dh else self.hi
        core = 1 - self.core if other_core else self.core
        return y * 4 + hi * 2 + core


def enter(me):
    barrier = pltpu.get_barrier_semaphore()

    def greet(j, carry):
        for device in ((me.f, lax.rem(me.s + j, N_SEQ)), (lax.rem(me.f + j, N_FSDP), me.s)):
            pl.semaphore_signal(barrier, inc=1, device_id=device, device_id_type=MESH)
        return carry

    lax.fori_loop(1, N_SEQ, greet, 0)
    pl.semaphore_wait(barrier, 2 * (N_SEQ - 1))


def remote(src, dst, send, recv, device):
    return pltpu.make_async_remote_copy(
        src_ref=src,
        dst_ref=dst,
        send_sem=send,
        recv_sem=recv,
        device_id=device,
        device_id_type=MESH,
    )


CHIP_PARTS = (
    ((-1, 0), (0, 3)),
    ((1, 0), (1, 4)),
    ((0, 1), (2, 5)),
    ((2, 0), (6, 7)),
    ((-1, 1), (8, 11)),
    ((1, 1), (9, 10)),
    ((2, 1), (12, 13, 14)),
)


def gather(
    me, x_hbm, g_hbm, wq_hbm, wk_hbm, wv_hbm, cos_hbm, sin_hbm,
    rows, q_ref, k_ref, v_ref, grad_ref, w_ref,
    cos_ref, sin_ref, x_send, x_recv, c_send, c_recv, g_send, g_recv, w_send, w_recv, l_sem,
):
    own = pl.multiple_of(me.s * ROWS, ROWS)
    head_col = pl.multiple_of(me.y * HEAD, HEAD)
    own_w = pl.ds(pl.multiple_of(me.f * ROWS, ROWS), ROWS)
    loads = [
        pltpu.make_async_copy(wq_hbm, w_ref.at[own_w, pl.ds(0, HEAD)], l_sem.at[0]),
        pltpu.make_async_copy(wk_hbm.at[:, pl.ds(head_col, HEAD)], w_ref.at[own_w, pl.ds(HEAD, HEAD)], l_sem.at[1]),
        pltpu.make_async_copy(wv_hbm.at[:, pl.ds(head_col, HEAD)], w_ref.at[own_w, pl.ds(HEAD, HEAD)], l_sem.at[1]),
        pltpu.make_async_copy(x_hbm, rows.at[pl.ds(own, ROWS), :], l_sem.at[2]),
        pltpu.make_async_copy(cos_hbm, cos_ref, l_sem.at[3]),
        pltpu.make_async_copy(sin_hbm, sin_ref, l_sem.at[4]),
        pltpu.make_async_copy(g_hbm.at[:, pl.ds(own, HEAD)], grad_ref.at[pl.ds(own, ROWS), :], l_sem.at[5]),
    ]
    loads[0].start()

    @pl.when(me.core == 0)
    def _():
        loads[1].start()

    @pl.when(me.core == 1)
    def _():
        loads[2].start()

    for load in loads[3:]:
        load.start()

    enter(me)

    def w_piece(lo, z):
        at = pl.multiple_of((lo * 8 + z) * ROWS, ROWS)
        return w_ref.at[pl.ds(at, ROWS), pl.ds(0, 2 * HEAD)]

    def w_copy(lo, z, slot, device):
        piece = w_piece(lo, z)
        return remote(piece, piece, w_send.at[slot], w_recv.at[slot], device)

    def w_push(j, other):
        lo = 1 - me.lo if other else me.lo
        return w_copy(lo, me.z, 8 * other + j, (me.lo * 8 + lax.rem(me.z + j, 8), me.s))

    def w_start(other):
        def step(j, carry):
            w_push(j, other).start()
            return carry

        lax.fori_loop(1, 8, step, 0)

    def w_finish(j, carry):
        back = lax.rem(me.z + 8 - j, 8)
        for other in (0, 1):
            lo = 1 - me.lo if other else me.lo
            w_copy(lo, back, 8 * other + j, me.to("lo")).wait_recv()
        return carry

    def w_sent(j, carry):
        for other in (0, 1):
            w_push(j, other).wait_send()
        return carry

    def part(rel, first, count, other_core=0):
        at = pl.multiple_of(me.block(rel, other_core) * ROWS + first, 16)
        return rows.at[pl.ds(at, count), :]

    def x_copy(i):
        direction, rel, first, count, _ = GATHER[i]
        piece = part(rel, first, count)
        source = x_hbm.at[pl.ds(first, count), :] if rel == (0, 0) else piece
        return remote(source, piece, x_send.at[i], x_recv.at[i], me.to(direction))

    def x_start(i):
        x_copy(i).start()

    def x_arrived(i):
        direction, _, first, count, rel = GATHER[i]
        piece = part(rel, first, count)
        remote(piece, piece, x_send.at[i], x_recv.at[i], me.to(direction)).wait_recv()
        core_copy(i).start()

    def core_copy(i, receive=False):
        rel, first, count = (0, 0), 0, 128
        if i < len(GATHER):
            _, _, first, count, rel = GATHER[i]
        piece = part(rel, first, count, other_core=1 if receive else 0)
        source = x_hbm if rel == (0, 0) and not receive else piece
        return remote(source, piece, c_send.at[i], c_recv.at[i], me.to("core"))

    def g_copy(j, device_s, source_s):
        at = pl.multiple_of(source_s * ROWS, ROWS)
        col = pl.multiple_of(device_s * HEAD, HEAD)
        return remote(
            g_hbm.at[:, pl.ds(col, HEAD)],
            grad_ref.at[pl.ds(at, ROWS), :],
            g_send.at[j],
            g_recv.at[j],
            (me.f, device_s),
        )

    def g_start(j, carry):
        g_copy(j, lax.rem(me.s + j, N_SEQ), me.s).start()
        return carry

    def project(rel, parts):
        for i in parts:
            core_copy(i, True).wait_recv()
        hi = 1 - me.hi if rel[1] else me.hi
        chip = lax.rem(me.y + rel[0] + 4, 4) * 2 + hi
        at = pl.ds(pl.multiple_of(chip * 256, 256), 256)
        full = jnp.dot(rows[at, :], w_ref[...], preferred_element_type=jnp.float32)
        cos, sin = cos_ref[at, :], sin_ref[at, :]
        q, first, second = full[:, :HEAD], full[:, HEAD : 2 * HEAD], full[:, 2 * HEAD :]
        is_key = me.core == 0
        k, v = jnp.where(is_key, first, second), jnp.where(is_key, second, first)
        q_ref[at, :] = (q * cos + pltpu.roll(q, HEAD // 2, 1) * sin).astype(jnp.bfloat16)
        k_ref[at, :] = (k * cos + pltpu.roll(k, HEAD // 2, 1) * sin).astype(jnp.bfloat16)
        v_ref[at, :] = v.astype(jnp.bfloat16)

    for i in range(6):
        x_start(i)
    loads[0].wait()
    loads[1].wait()
    own_to_lo = w_copy(me.lo, me.z, 0, me.to("lo"))
    own_to_lo.start()
    w_start(0)
    core_copy(len(GATHER)).start()
    w_copy(1 - me.lo, me.z, 0, me.to("lo")).wait_recv()
    w_start(1)
    x_arrived(0)
    x_start(6)
    x_start(8)
    x_arrived(1)
    x_start(7)
    x_start(9)
    x_arrived(2)
    x_start(10)
    x_arrived(5)
    x_start(11)
    x_arrived(3)
    x_arrived(4)
    x_arrived(8)
    x_start(12)
    x_arrived(9)
    x_start(13)
    x_arrived(6)
    x_arrived(7)
    x_start(14)
    lax.fori_loop(1, N_SEQ, g_start, 0)
    for load in loads[3:]:
        load.wait()
    lax.fori_loop(1, 8, w_finish, 0)
    share = remote(
        w_ref.at[:, pl.ds(HEAD, HEAD)],
        w_ref.at[:, pl.ds(2 * HEAD, HEAD)],
        w_send.at[8],
        w_recv.at[8],
        me.to("core"),
    )
    share.start()
    share.wait_recv()
    project((0, 0), (len(GATHER),))
    for rel, parts in CHIP_PARTS[:4]:
        project(rel, parts)
    x_arrived(10)
    x_arrived(11)
    for rel, parts in CHIP_PARTS[4:6]:
        project(rel, parts)
    for i in CHIP_PARTS[6][1]:
        x_arrived(i)
    project(*CHIP_PARTS[6])

    def g_finish(j, carry):
        back = lax.rem(me.s + N_SEQ - j, N_SEQ)
        g_copy(j, back, back).wait_recv()
        g_copy(j, lax.rem(me.s + j, N_SEQ), me.s).wait_send()
        return carry

    lax.fori_loop(1, N_SEQ, g_finish, 0)
    share.wait_send()
    own_to_lo.wait_send()
    lax.fori_loop(1, 8, w_sent, 0)
    for i in range(len(GATHER)):
        x_copy(i).wait_send()
    for i in range(len(GATHER) + 1):
        core_copy(i).wait_send()


NT = (((1,), (1,)), ((), ()))
TN = (((0,), (0,)), ((), ()))
QB = 256


def attention(me, b_ref, q_ref, k_ref, v_ref, g_ref, cos_ref, sin_ref, out_ref, sc, dp_sc, dk_sc, dv_sc, kt_sc):
    start = b_ref[0]
    kt_sc[...] = k_ref[...].T
    for i in range(LENGTH // QB):
        rows_i = pl.ds(i * QB, QB)
        q = q_ref[rows_i, :]
        g = g_ref[rows_i, :]
        q_pos = i * QB + lax.broadcasted_iota(jnp.int32, (1, QB), 1)
        low = jnp.where(q_pos < start, 0, start)
        top = jnp.full((1, QB), -1e30, jnp.float32)
        for j in range(i + 1):
            at = pl.ds(j * QB, QB)
            s = lax.dot_general(k_ref[at, :], q, NT, preferred_element_type=jnp.float32)
            k_pos = j * QB + lax.broadcasted_iota(jnp.int32, (QB, QB), 0)
            ok = k_pos >= low
            if j == i:
                ok = ok & (k_pos <= q_pos)
            s = jnp.where(ok, s, -1e30)
            sc[at, :] = s
            top = jnp.maximum(top, jnp.max(s, axis=0, keepdims=True))
        top = top * EXP2_SCALE
        total = jnp.zeros((1, QB), jnp.float32)
        for j in range(i + 1):
            at = pl.ds(j * QB, QB)
            e = jnp.exp2(sc[at, :] * EXP2_SCALE - top)
            sc[at, :] = e
            total = total + jnp.sum(e, axis=0, keepdims=True)
        inverse = 1.0 / total
        delta = jnp.zeros((1, QB), jnp.float32)
        for j in range(i + 1):
            at = pl.ds(j * QB, QB)
            p = sc[at, :] * inverse
            sc[at, :] = p
            low_p = p.astype(jnp.bfloat16)
            d = lax.dot_general(v_ref[at, :], g, NT, preferred_element_type=jnp.float32)
            dp_sc[at, :] = d
            delta = delta + jnp.sum(low_p.astype(jnp.float32) * d, axis=0, keepdims=True)
            dv = jnp.dot(low_p, g, preferred_element_type=jnp.float32)
            if j == i:
                dv_sc[at, :] = dv
            else:
                dv_sc[at, :] += dv
        dq = jnp.zeros((HEAD, QB), jnp.float32)
        for j in range(i + 1):
            at = pl.ds(j * QB, QB)
            ds = (sc[at, :] * (dp_sc[at, :] - delta)).astype(jnp.bfloat16)
            dk = jnp.dot(ds, q, preferred_element_type=jnp.float32)
            if j == i:
                dk_sc[at, :] = dk
            else:
                dk_sc[at, :] += dk
            dq = dq + jnp.dot(kt_sc[:, at], ds, preferred_element_type=jnp.float32)
        dq = dq.T * SCALE
        out_ref[rows_i, :HEAD] = (
            dq * cos_ref[rows_i, :] - pltpu.roll(dq, HEAD // 2, 1) * sin_ref[rows_i, :]
        ).astype(jnp.bfloat16)

    key_col = pl.ds(pl.multiple_of(HEAD + me.core * HEAD, HEAD), HEAD)
    value_col = pl.ds(pl.multiple_of(2 * HEAD - me.core * HEAD, HEAD), HEAD)

    def finish(c, carry):
        at = pl.ds(pl.multiple_of(c * QB, QB), QB)
        dk = dk_sc[at, :] * SCALE
        out_ref[at, key_col] = (
            dk * cos_ref[at, :] - pltpu.roll(dk, HEAD // 2, 1) * sin_ref[at, :]
        ).astype(jnp.bfloat16)
        out_ref[at, value_col] = dv_sc[at, :].astype(jnp.bfloat16)
        return carry

    lax.fori_loop(0, LENGTH // QB, finish, 0)


ORDER = ((2, 1), (-1, 1), (1, 1), (2, 0), (0, 1), (-1, 0), (1, 0), (0, 0))
SLOT = {rel: n for n, rel in enumerate(ORDER)}
RECV_AT = []
_at = 0
for _piece in REDUCE:
    RECV_AT.append(_at)
    _at += _piece[3]
RECV_ROWS = _at


def scatter(
    me, g_ref, w_ref, rows, in_ref, dq_ref, dk_ref, dv_ref,
    mine, away, near, arrived, dwq, dwm, dwo, kv_near, f_in, kv_all,
    r_send, r_recv, n_send, n_recv, kv_sem, f_send, f_recv, a_send, a_recv,
):
    def partial_sum(rel, other_core):
        at = pl.ds(pl.multiple_of(me.block(rel, other_core) * ROWS, ROWS), ROWS)
        return lax.dot_general(
            g_ref[at, :], w_ref[...], NT, preferred_element_type=jnp.float32
        ).astype(jnp.bfloat16)

    def near_copy(n):
        return remote(away.at[n], near.at[n], n_send.at[n], n_recv.at[n], me.to("core"))

    def block_out(rel):
        n = SLOT[rel]
        away[n] = partial_sum(rel, 1)
        near_copy(n).start()
        mine[n] = partial_sum(rel, 0)

    def block_in(rel):
        n = SLOT[rel]
        near_copy(n).wait_recv()
        mine[n] = (mine[n].astype(jnp.float32) + near[n].astype(jnp.float32)).astype(jnp.bfloat16)

    def r_copy(i):
        direction, rel, first, count, _ = REDUCE[i]
        return remote(
            mine.at[SLOT[rel], pl.ds(first, count), :],
            arrived.at[pl.ds(RECV_AT[i], count), :],
            r_send.at[i],
            r_recv.at[i],
            me.to(direction),
        )

    def r_add(i):
        _, _, first, count, rel = REDUCE[i]
        r_copy(i).wait_recv()
        n = SLOT[rel]
        mine[n, pl.ds(first, count), :] = (
            mine[n, pl.ds(first, count), :].astype(jnp.float32)
            + arrived[pl.ds(RECV_AT[i], count), :].astype(jnp.float32)
        ).astype(jnp.bfloat16)

    def weights(first_col, count, targets):
        def step(c, carry):
            at = pl.ds(pl.multiple_of(c * 512, 512), 512)
            part = lax.dot_general(
                g_ref[:, pl.ds(first_col, count)], rows[:, at], TN, preferred_element_type=jnp.float32
            ).astype(jnp.bfloat16)
            for n, target in enumerate(targets):
                for k in range(4):
                    target[c * 4 + k] = part[n * HEAD : (n + 1) * HEAD, k * ROWS : (k + 1) * ROWS]
            return carry

        lax.fori_loop(0, FEATURES // 512, step, 0)

    kv_copy = remote(dwo, kv_near, kv_sem.at[0], kv_sem.at[1], me.to("core"))

    def f_copy(source, kind, j):
        to = lax.rem(me.f + j, N_FSDP)
        return remote(source.at[to], f_in.at[kind, j], f_send.at[kind, j], f_recv.at[kind, j], (to, me.s))

    def f_start(source, kind):
        def step(j, carry):
            f_copy(source, kind, j).start()
            return carry

        lax.fori_loop(1, N_FSDP, step, 0)

    def f_sum(source, kind):
        def step(j, total):
            f_copy(source, kind, j).wait()
            return total + f_in[kind, j].astype(jnp.float32)

        return lax.fori_loop(1, N_FSDP, step, source[me.f].astype(jnp.float32))

    chip = lax.div(me.s, 2)

    def a_copy(j, source):
        slot = kv_all.at[me.core, source]
        to = (me.f, lax.rem(me.s + 2 * j, N_SEQ))
        return remote(slot, slot, a_send.at[j], a_recv.at[j], to)

    def a_start(j, carry):
        a_copy(j, chip).start()
        return carry

    def a_arrived(j, carry):
        a_copy(j, lax.rem(chip + 8 - j, 8)).wait_recv()
        return carry

    def a_sent(j, carry):
        a_copy(j, chip).wait_send()
        return carry

    def r_start(*pieces):
        for i in pieces:
            r_copy(i).start()

    block_out((2, 1))
    block_out((-1, 1))
    block_in((2, 1))
    r_start(0, 1, 2)
    block_out((1, 1))
    block_in((-1, 1))
    r_start(3)
    weights(HEAD, 2 * HEAD, (dwm, dwo))
    kv_copy.start()
    block_in((1, 1))
    r_start(4)
    block_out((2, 0))
    weights(0, HEAD, (dwq,))
    f_start(dwq, 0)
    kv_copy.wait_recv()

    def kv_add(c, carry):
        dwm[c] = (dwm[c].astype(jnp.float32) + kv_near[c].astype(jnp.float32)).astype(jnp.bfloat16)
        return carry

    lax.fori_loop(0, N_FSDP, kv_add, 0)
    f_start(dwm, 1)
    r_add(0)
    r_start(5)
    r_add(1)
    r_start(6)
    block_in((2, 0))
    r_add(2)
    r_start(7, 8)
    block_out((-1, 0))
    block_out((1, 0))
    block_in((-1, 0))
    r_start(9)
    block_in((1, 0))
    r_start(10)
    block_out((0, 1))
    block_out((0, 0))
    block_in((0, 1))
    r_add(3)
    r_add(4)
    r_start(11, 12)
    block_in((0, 0))
    r_add(5)
    r_add(7)
    r_start(13)
    r_add(6)
    r_add(8)
    r_start(14)
    kv_all[me.core, chip] = f_sum(dwm, 1).astype(jnp.bfloat16)
    lax.fori_loop(1, 8, a_start, 0)
    dq_ref[...] = f_sum(dwq, 0).T
    lax.fori_loop(1, 8, a_arrived, 0)
    kv_mine, kv_theirs = kv_all.at[me.core], kv_all.at[1 - me.core]
    kv_share = remote(kv_mine, kv_mine, kv_sem.at[2], kv_sem.at[3], me.to("core"))
    kv_share.start()
    for first, pieces in LAST:
        total = mine[SLOT[(0, 0)], pl.ds(first, 64), :].astype(jnp.float32)
        for i in pieces:
            r_copy(i).wait_recv()
            total = total + arrived[pl.ds(RECV_AT[i], 64), :].astype(jnp.float32)
        in_ref[pl.ds(first, 64), :] = total.astype(jnp.bfloat16)
    remote(kv_theirs, kv_theirs, kv_sem.at[2], kv_sem.at[3], me.to("core")).wait_recv()
    for n in range(4):
        at = pl.ds(n * HEAD, HEAD)
        for kind, out in ((0, dk_ref), (1, dv_ref)):
            out[:, at] = (
                kv_all[kind, 2 * n].astype(jnp.float32) + kv_all[kind, 2 * n + 1].astype(jnp.float32)
            ).T
    lax.fori_loop(1, 8, a_sent, 0)
    kv_share.wait_send()
    kv_copy.wait_send()
    for i in range(len(REDUCE)):
        r_copy(i).wait_send()
    for n in range(len(ORDER)):
        near_copy(n).wait_send()


def whole_kernel(
    x_hbm, g_hbm, wq_hbm, wk_hbm, wv_hbm, cos_hbm, sin_hbm, b_ref,
    in_ref, dq_ref, dk_ref, dv_ref,
    rows, q_ref, k_ref, v_ref, grad_ref, w_ref, cos_ref, sin_ref,
    sc, dp_sc, dk_sc, dv_sc, kt_sc, cols,
    mine, away, near, arrived, dwq, dwm, dwo, kv_near, f_in, kv_all,
    *sems,
):
    me = Place()
    gather(
        me, x_hbm, g_hbm, wq_hbm, wk_hbm, wv_hbm, cos_hbm, sin_hbm,
        rows, q_ref, k_ref, v_ref, grad_ref, w_ref, cos_ref, sin_ref, *sems[:9],
    )
    attention(me, b_ref, q_ref, k_ref, v_ref, grad_ref, cos_ref, sin_ref, cols, sc, dp_sc, dk_sc, dv_sc, kt_sc)
    scatter(
        me, cols, w_ref, rows, in_ref, dq_ref, dk_ref, dv_ref,
        mine, away, near, arrived, dwq, dwm, dwo, kv_near, f_in, kv_all, *sems[9:],
    )


def rope_tables():
    half = HEAD // 2
    inverse = (500000.0 ** (-(np.arange(half, dtype=np.float64) * 2.0 / HEAD))).astype(np.float32)
    angles = np.arange(LENGTH, dtype=np.float32)[:, None] * inverse[None, :]
    cos, sin = np.cos(angles), np.sin(angles)
    return np.concatenate([cos, cos], axis=1), np.concatenate([-sin, sin], axis=1)


def vmem():
    return pl.BlockSpec(memory_space=pltpu.VMEM)


BF16, F32 = jnp.bfloat16, jnp.float32
dma = pltpu.SemaphoreType.DMA
shape = jax.ShapeDtypeStruct
VMEM_LIMIT = 62 * 2**20


def run(x, g, wq, wk, wv, cos, sin, boundary):
    per_head = pltpu.VMEM((LENGTH, HEAD), BF16)
    table = pltpu.VMEM((LENGTH, HEAD), F32)
    scores = pltpu.VMEM((LENGTH, QB), F32)
    blocks = pltpu.VMEM((8, ROWS, FEATURES), BF16)
    pieces = pltpu.VMEM((N_FSDP, HEAD, ROWS), BF16)
    hbm = pl.BlockSpec(memory_space=pltpu.HBM)
    return pl.pallas_call(
        whole_kernel,
        out_shape=(
            shape((ROWS, FEATURES), BF16),
            shape((ROWS, HEAD), F32),
            shape((ROWS, GROUP * HEAD), F32),
            shape((ROWS, GROUP * HEAD), F32),
        ),
        in_specs=[hbm] * 7 + [pl.BlockSpec(memory_space=pltpu.SMEM)],
        out_specs=(vmem(),) * 4,
        scratch_shapes=[
            pltpu.VMEM((LENGTH, FEATURES), BF16),
            per_head,
            per_head,
            per_head,
            per_head,
            pltpu.VMEM((FEATURES, 3 * HEAD), BF16),
            table,
            table,
            scores,
            scores,
            table,
            table,
            pltpu.VMEM((HEAD, LENGTH), BF16),
            pltpu.VMEM((LENGTH, 3 * HEAD), BF16),
            blocks,
            blocks,
            blocks,
            pltpu.VMEM((RECV_ROWS, FEATURES), BF16),
            pieces,
            pieces,
            pieces,
            pieces,
            pltpu.VMEM((2, N_FSDP, HEAD, ROWS), BF16),
            pltpu.VMEM((2, 8, HEAD, ROWS), BF16),
            dma((len(GATHER),)),
            dma((len(GATHER),)),
            dma((len(GATHER) + 1,)),
            dma((len(GATHER) + 1,)),
            dma((N_SEQ,)),
            dma((N_SEQ,)),
            dma((16,)),
            dma((16,)),
            dma((6,)),
            dma((len(REDUCE),)),
            dma((len(REDUCE),)),
            dma((len(ORDER),)),
            dma((len(ORDER),)),
            dma((4,)),
            dma((2, N_FSDP)),
            dma((2, N_FSDP)),
            dma((8,)),
            dma((8,)),
        ],
        compiler_params=pltpu.CompilerParams(collective_id=1, has_side_effects=True, vmem_limit_bytes=VMEM_LIMIT),
        name="attention_backward",
    )(x, g, wq, wk, wv, cos, sin, boundary)


def shards(normed_input, out_grad, w_query, key_weight_matrix, value_weight_matrix, boundary):
    cos, sin = rope_tables()
    input_grad, dq, dk, dv = run(
        normed_input[0], out_grad[0], w_query, key_weight_matrix, value_weight_matrix,
        jnp.asarray(cos), jnp.asarray(sin), boundary,
    )
    return (input_grad[None], dq, dk, dv)


def solution(mesh):
    return jax.shard_map(
        shards,
        mesh=mesh,
        in_specs=(
            P("fsdp", "seq", None),
            P("fsdp", "seq", None),
            P("fsdp", "seq"),
            P("fsdp", None),
            P("fsdp", None),
            P("fsdp"),
        ),
        out_specs=(P("fsdp", "seq", None), P("fsdp", "seq"), P("fsdp", None), P("fsdp", None)),
        check_vma=False,
    )
```

```python
import jax
import jax.numpy as jnp
import numpy as np
from jax import lax
from jax.experimental import pallas as pl
from jax.experimental.pallas import tpu as pltpu
from jax.sharding import PartitionSpec as P

HEAD = 128
N_SEQ = 16
N_FSDP = 16
ROWS = 128
LENGTH = 2048
FEATURES = 2048
GROUP = 4
MESH = pl.DeviceIdType.MESH
SCALE = HEAD ** (-0.5)
EXP2_SCALE = SCALE * 1.4426950408889634

GATHER = (
    ("up", (0, 0), 0, 64, (-1, 0)),
    ("down", (0, 0), 64, 64, (1, 0)),
    ("side", (0, 0), 0, 64, (0, 1)),
    ("up", (0, 0), 64, 64, (-1, 0)),
    ("down", (0, 0), 0, 64, (1, 0)),
    ("side", (0, 0), 64, 64, (0, 1)),
    ("up", (-1, 0), 0, 64, (2, 0)),
    ("down", (1, 0), 64, 64, (2, 0)),
    ("side", (-1, 0), 0, 48, (-1, 1)),
    ("side", (1, 0), 80, 48, (1, 1)),
    ("down", (0, 1), 0, 64, (1, 1)),
    ("up", (0, 1), 64, 64, (-1, 1)),
    ("up", (-1, 1), 0, 48, (2, 1)),
    ("down", (1, 1), 80, 48, (2, 1)),
    ("side", (2, 0), 48, 32, (2, 1)),
    ("side", (-1, 0), 48, 16, (-1, 1)),
    ("side", (1, 0), 64, 16, (1, 1)),
)

REDUCE = (
    ("down", (2, 1), 0, 48, (-1, 1)),
    ("up", (2, 1), 80, 48, (1, 1)),
    ("side", (2, 1), 48, 32, (2, 0)),
    ("down", (-1, 1), 64, 64, (0, 1)),
    ("up", (1, 1), 0, 64, (0, 1)),
    ("side", (-1, 1), 48, 16, (-1, 0)),
    ("side", (1, 1), 64, 16, (1, 0)),
    ("side", (-1, 1), 0, 48, (-1, 0)),
    ("side", (1, 1), 80, 48, (1, 0)),
    ("down", (2, 0), 0, 64, (-1, 0)),
    ("up", (2, 0), 64, 64, (1, 0)),
    ("down", (-1, 0), 64, 64, (0, 0)),
    ("up", (1, 0), 0, 64, (0, 0)),
    ("side", (0, 1), 0, 64, (0, 0)),
    ("side", (0, 1), 64, 64, (0, 0)),
    ("down", (-1, 0), 0, 64, (0, 0)),
    ("up", (1, 0), 64, 64, (0, 0)),
)
LAST = ((0, (12, 13, 15)), (64, (11, 14, 16)))


class Place:
    def __init__(self):
        self.f = lax.axis_index("fsdp")
        self.s = lax.axis_index("seq")
        self.core = lax.rem(self.s, 2)
        self.hi = lax.rem(lax.div(self.s, 2), 2)
        self.y = lax.div(self.s, 4)
        self.z = lax.rem(self.f, 8)
        self.lo = lax.div(self.f, 8)

    def to(self, direction):
        s = self.s
        if direction == "up":
            return (self.f, lax.rem(s + 4, N_SEQ))
        if direction == "down":
            return (self.f, lax.rem(s + 12, N_SEQ))
        if direction == "side":
            return (self.f, s + 2 - 4 * self.hi)
        if direction == "lo":
            return ((1 - self.lo) * 8 + self.z, s)
        return (self.f, s + 1 - 2 * self.core)

    def block(self, rel, other_core=0):
        dy, dh = rel
        y = lax.rem(self.y + dy + 4, 4)
        hi = 1 - self.hi if dh else self.hi
        core = 1 - self.core if other_core else self.core
        return y * 4 + hi * 2 + core


def enter(me):
    barrier = pltpu.get_barrier_semaphore()

    def greet(device):
        pl.semaphore_signal(barrier, inc=1, device_id=device, device_id_type=MESH)

    def greet_seq(j, carry):
        greet((me.f, lax.rem(me.s + j, N_SEQ)))
        return carry

    def greet_z(j, carry):
        greet((me.lo * 8 + lax.rem(me.z + j, 8), me.s))
        return carry

    lax.fori_loop(1, N_SEQ, greet_seq, 0)
    lax.fori_loop(1, 8, greet_z, 0)
    greet(me.to("lo"))
    pl.semaphore_wait(barrier, N_SEQ - 1 + 8)


def remote(src, dst, send, recv, device):
    return pltpu.make_async_remote_copy(
        src_ref=src,
        dst_ref=dst,
        send_sem=send,
        recv_sem=recv,
        device_id=device,
        device_id_type=MESH,
    )


CHIP_PARTS = (
    ((-1, 0), (0, 3)),
    ((1, 0), (1, 4)),
    ((0, 1), (2, 5)),
    ((2, 0), (6, 7)),
    ((-1, 1), (8, 11, 15)),
    ((1, 1), (9, 10, 16)),
    ((2, 1), (12, 13, 14)),
)


def gather(
    me, x_hbm, g_hbm, wq_hbm, wk_hbm, wv_hbm, cos_hbm, sin_hbm,
    rows, q_ref, k_ref, v_ref, grad_ref, w_ref,
    cos_ref, sin_ref, x_send, x_recv, c_send, c_recv, g_send, g_recv, w_send, w_recv, l_sem,
):
    own = pl.multiple_of(me.s * ROWS, ROWS)
    head_col = pl.multiple_of(me.y * HEAD, HEAD)
    own_w = pl.ds(pl.multiple_of(me.f * ROWS, ROWS), ROWS)
    loads = [
        pltpu.make_async_copy(wq_hbm, w_ref.at[own_w, pl.ds(0, HEAD)], l_sem.at[0]),
        pltpu.make_async_copy(wk_hbm.at[:, pl.ds(head_col, HEAD)], w_ref.at[own_w, pl.ds(HEAD, HEAD)], l_sem.at[1]),
        pltpu.make_async_copy(wv_hbm.at[:, pl.ds(head_col, HEAD)], w_ref.at[own_w, pl.ds(HEAD, HEAD)], l_sem.at[1]),
        pltpu.make_async_copy(x_hbm, rows.at[pl.ds(own, ROWS), :], l_sem.at[2]),
        pltpu.make_async_copy(cos_hbm, cos_ref, l_sem.at[3]),
        pltpu.make_async_copy(sin_hbm, sin_ref, l_sem.at[4]),
        pltpu.make_async_copy(g_hbm.at[:, pl.ds(own, HEAD)], grad_ref.at[pl.ds(own, ROWS), :], l_sem.at[5]),
    ]
    loads[0].start()

    @pl.when(me.core == 0)
    def _():
        loads[1].start()

    @pl.when(me.core == 1)
    def _():
        loads[2].start()

    for load in loads[3:]:
        load.start()

    enter(me)

    def w_piece(lo, z):
        at = pl.multiple_of((lo * 8 + z) * ROWS, ROWS)
        return w_ref.at[pl.ds(at, ROWS), pl.ds(0, 2 * HEAD)]

    def w_copy(lo, z, slot, device):
        piece = w_piece(lo, z)
        return remote(piece, piece, w_send.at[slot], w_recv.at[slot], device)

    def along(dz):
        return (me.lo * 8 + lax.rem(me.z + dz + 8, 8), me.s)

    def w_move(other, held, hop):
        lo = 1 - me.lo if other else me.lo
        return w_copy(lo, lax.rem(me.z + held + 8, 8), 9 * other + 4 + hop - held, along(hop))

    def w_arrival(other, away):
        lo = 1 - me.lo if other else me.lo
        return w_copy(lo, lax.rem(me.z + away + 8, 8), 9 * other + 4 - away, along(1))

    first_moves = [(0, hop) for hop in (1, -1, 2, -2)]
    next_moves = {0: ((-2, 1), (2, -1), (-2, 2)), 1: ((-2, 1), (2, -1), (2, -2))}

    def w_start(other):
        for held, hop in first_moves:
            w_move(other, held, hop).start()

    def w_onward(other):
        w_arrival(other, -2).wait_recv()
        w_arrival(other, 2).wait_recv()
        for held, hop in next_moves[other]:
            w_move(other, held, hop).start()

    def w_finish():
        for other in (0, 1):
            for away in (-1, 1, -3, 3, -4 if other == 0 else 4):
                w_arrival(other, away).wait_recv()

    def w_sent():
        for other in (0, 1):
            for held, hop in first_moves + list(next_moves[other]):
                w_move(other, held, hop).wait_send()

    def part(rel, first, count, other_core=0):
        at = pl.multiple_of(me.block(rel, other_core) * ROWS + first, 16)
        return rows.at[pl.ds(at, count), :]

    def x_copy(i):
        direction, rel, first, count, _ = GATHER[i]
        piece = part(rel, first, count)
        source = x_hbm.at[pl.ds(first, count), :] if rel == (0, 0) else piece
        return remote(source, piece, x_send.at[i], x_recv.at[i], me.to(direction))

    def x_start(i):
        x_copy(i).start()

    def x_arrived(i):
        direction, _, first, count, rel = GATHER[i]
        piece = part(rel, first, count)
        remote(piece, piece, x_send.at[i], x_recv.at[i], me.to(direction)).wait_recv()
        core_copy(i).start()

    def core_copy(i, receive=False):
        rel, first, count = (0, 0), 0, 128
        if i < len(GATHER):
            _, _, first, count, rel = GATHER[i]
        piece = part(rel, first, count, other_core=1 if receive else 0)
        source = x_hbm if rel == (0, 0) and not receive else piece
        return remote(source, piece, c_send.at[i], c_recv.at[i], me.to("core"))

    def g_copy(j, device_s, source_s):
        at = pl.multiple_of(source_s * ROWS, ROWS)
        col = pl.multiple_of(device_s * HEAD, HEAD)
        return remote(
            g_hbm.at[:, pl.ds(col, HEAD)],
            grad_ref.at[pl.ds(at, ROWS), :],
            g_send.at[j],
            g_recv.at[j],
            (me.f, device_s),
        )

    def g_start(j, carry):
        g_copy(j, lax.rem(me.s + j, N_SEQ), me.s).start()
        return carry

    def project(rel, parts):
        for i in parts:
            core_copy(i, True).wait_recv()
        hi = 1 - me.hi if rel[1] else me.hi
        chip = lax.rem(me.y + rel[0] + 4, 4) * 2 + hi
        at = pl.ds(pl.multiple_of(chip * 256, 256), 256)
        full = jnp.dot(rows[at, :], w_ref[...], preferred_element_type=jnp.float32)
        cos, sin = cos_ref[at, :], sin_ref[at, :]
        q, first, second = full[:, :HEAD], full[:, HEAD : 2 * HEAD], full[:, 2 * HEAD :]
        is_key = me.core == 0
        k, v = jnp.where(is_key, first, second), jnp.where(is_key, second, first)
        q_ref[at, :] = (q * cos + pltpu.roll(q, HEAD // 2, 1) * sin).astype(jnp.bfloat16)
        k_ref[at, :] = (k * cos + pltpu.roll(k, HEAD // 2, 1) * sin).astype(jnp.bfloat16)
        v_ref[at, :] = v.astype(jnp.bfloat16)

    for i in range(6):
        x_start(i)
    loads[0].wait()
    loads[1].wait()
    own_to_lo = w_copy(me.lo, me.z, 4, me.to("lo"))
    own_to_lo.start()
    w_start(0)
    core_copy(len(GATHER)).start()
    w_copy(1 - me.lo, me.z, 4, me.to("lo")).wait_recv()
    w_start(1)
    x_arrived(0)
    x_start(6)
    x_start(8)
    x_arrived(1)
    x_start(7)
    x_start(9)
    x_start(15)
    x_start(16)
    x_arrived(2)
    x_start(10)
    w_onward(0)
    w_onward(1)
    x_arrived(5)
    x_start(11)
    x_arrived(3)
    x_arrived(4)
    x_arrived(8)
    x_start(12)
    x_arrived(9)
    x_start(13)
    x_arrived(6)
    x_arrived(7)
    x_start(14)
    lax.fori_loop(1, N_SEQ, g_start, 0)
    for load in loads[3:]:
        load.wait()
    w_finish()
    share = remote(
        w_ref.at[:, pl.ds(HEAD, HEAD)],
        w_ref.at[:, pl.ds(2 * HEAD, HEAD)],
        w_send.at[17],
        w_recv.at[17],
        me.to("core"),
    )
    share.start()
    share.wait_recv()
    project((0, 0), (len(GATHER),))
    for rel, parts in CHIP_PARTS[:4]:
        project(rel, parts)
    x_arrived(10)
    x_arrived(11)
    x_arrived(15)
    x_arrived(16)
    for rel, parts in CHIP_PARTS[4:6]:
        project(rel, parts)
    for i in CHIP_PARTS[6][1]:
        x_arrived(i)
    project(*CHIP_PARTS[6])

    def g_finish(j, carry):
        back = lax.rem(me.s + N_SEQ - j, N_SEQ)
        g_copy(j, back, back).wait_recv()
        g_copy(j, lax.rem(me.s + j, N_SEQ), me.s).wait_send()
        return carry

    lax.fori_loop(1, N_SEQ, g_finish, 0)
    share.wait_send()
    own_to_lo.wait_send()
    w_sent()
    for i in range(len(GATHER)):
        x_copy(i).wait_send()
    for i in range(len(GATHER) + 1):
        core_copy(i).wait_send()


NT = (((1,), (1,)), ((), ()))
TN = (((0,), (0,)), ((), ()))
QB = 256


def attention(me, b_ref, q_ref, k_ref, v_ref, g_ref, cos_ref, sin_ref, out_ref, sc, dp_sc, dk_sc, dv_sc, kt_sc):
    start = b_ref[0]
    kt_sc[...] = k_ref[...].T
    for i in range(LENGTH // QB):
        rows_i = pl.ds(i * QB, QB)
        q = q_ref[rows_i, :]
        g = g_ref[rows_i, :]
        q_pos = i * QB + lax.broadcasted_iota(jnp.int32, (1, QB), 1)
        low = jnp.where(q_pos < start, 0, start)
        top = jnp.full((1, QB), -1e30, jnp.float32)
        for j in range(i + 1):
            at = pl.ds(j * QB, QB)
            s = lax.dot_general(k_ref[at, :], q, NT, preferred_element_type=jnp.float32)
            k_pos = j * QB + lax.broadcasted_iota(jnp.int32, (QB, QB), 0)
            ok = k_pos >= low
            if j == i:
                ok = ok & (k_pos <= q_pos)
            s = jnp.where(ok, s, -1e30)
            sc[at, :] = s
            top = jnp.maximum(top, jnp.max(s, axis=0, keepdims=True))
        top = top * EXP2_SCALE
        total = jnp.zeros((1, QB), jnp.float32)
        for j in range(i + 1):
            at = pl.ds(j * QB, QB)
            e = jnp.exp2(sc[at, :] * EXP2_SCALE - top)
            sc[at, :] = e
            total = total + jnp.sum(e, axis=0, keepdims=True)
        inverse = 1.0 / total
        delta = jnp.zeros((1, QB), jnp.float32)
        for j in range(i + 1):
            at = pl.ds(j * QB, QB)
            p = sc[at, :] * inverse
            sc[at, :] = p
            low_p = p.astype(jnp.bfloat16)
            d = lax.dot_general(v_ref[at, :], g, NT, preferred_element_type=jnp.float32)
            dp_sc[at, :] = d
            delta = delta + jnp.sum(low_p.astype(jnp.float32) * d, axis=0, keepdims=True)
            dv = jnp.dot(low_p, g, preferred_element_type=jnp.float32)
            if j == i:
                dv_sc[at, :] = dv
            else:
                dv_sc[at, :] += dv
        dq = jnp.zeros((HEAD, QB), jnp.float32)
        for j in range(i + 1):
            at = pl.ds(j * QB, QB)
            ds = (sc[at, :] * (dp_sc[at, :] - delta)).astype(jnp.bfloat16)
            dk = jnp.dot(ds, q, preferred_element_type=jnp.float32)
            if j == i:
                dk_sc[at, :] = dk
            else:
                dk_sc[at, :] += dk
            dq = dq + jnp.dot(kt_sc[:, at], ds, preferred_element_type=jnp.float32)
        dq = dq.T * SCALE
        out_ref[rows_i, :HEAD] = (
            dq * cos_ref[rows_i, :] - pltpu.roll(dq, HEAD // 2, 1) * sin_ref[rows_i, :]
        ).astype(jnp.bfloat16)

    key_col = pl.ds(pl.multiple_of(HEAD + me.core * HEAD, HEAD), HEAD)
    value_col = pl.ds(pl.multiple_of(2 * HEAD - me.core * HEAD, HEAD), HEAD)

    def finish(c, carry):
        at = pl.ds(pl.multiple_of(c * QB, QB), QB)
        dk = dk_sc[at, :] * SCALE
        out_ref[at, key_col] = (
            dk * cos_ref[at, :] - pltpu.roll(dk, HEAD // 2, 1) * sin_ref[at, :]
        ).astype(jnp.bfloat16)
        out_ref[at, value_col] = dv_sc[at, :].astype(jnp.bfloat16)
        return carry

    lax.fori_loop(0, LENGTH // QB, finish, 0)


ORDER = ((2, 1), (-1, 1), (1, 1), (2, 0), (0, 1), (-1, 0), (1, 0), (0, 0))
SLOT = {rel: n for n, rel in enumerate(ORDER)}
RECV_AT = []
_at = 0
for _piece in REDUCE:
    RECV_AT.append(_at)
    _at += _piece[3]
RECV_ROWS = _at


def scatter(
    me, g_ref, w_ref, rows, in_ref, dq_ref, dk_ref, dv_ref,
    mine, away, near, arrived, dwq, dwm, dwo, kv_near, f_in, lo_out, lo_in, kv_all,
    r_send, r_recv, n_send, n_recv, kv_sem, f_send, f_recv, a_send, a_recv,
):
    def partial_sum(rel, other_core):
        at = pl.ds(pl.multiple_of(me.block(rel, other_core) * ROWS, ROWS), ROWS)
        return lax.dot_general(
            g_ref[at, :], w_ref[...], NT, preferred_element_type=jnp.float32
        ).astype(jnp.bfloat16)

    def near_copy(n):
        return remote(away.at[n], near.at[n], n_send.at[n], n_recv.at[n], me.to("core"))

    def block_out(rel):
        n = SLOT[rel]
        away[n] = partial_sum(rel, 1)
        near_copy(n).start()
        mine[n] = partial_sum(rel, 0)

    def block_in(rel):
        n = SLOT[rel]
        near_copy(n).wait_recv()
        mine[n] = (mine[n].astype(jnp.float32) + near[n].astype(jnp.float32)).astype(jnp.bfloat16)

    def r_copy(i):
        direction, rel, first, count, _ = REDUCE[i]
        return remote(
            mine.at[SLOT[rel], pl.ds(first, count), :],
            arrived.at[pl.ds(RECV_AT[i], count), :],
            r_send.at[i],
            r_recv.at[i],
            me.to(direction),
        )

    def r_add(i):
        _, _, first, count, rel = REDUCE[i]
        r_copy(i).wait_recv()
        n = SLOT[rel]
        mine[n, pl.ds(first, count), :] = (
            mine[n, pl.ds(first, count), :].astype(jnp.float32)
            + arrived[pl.ds(RECV_AT[i], count), :].astype(jnp.float32)
        ).astype(jnp.bfloat16)

    def weights(first_col, count, targets):
        def step(c, carry):
            at = pl.ds(pl.multiple_of(c * 512, 512), 512)
            part = lax.dot_general(
                g_ref[:, pl.ds(first_col, count)], rows[:, at], TN, preferred_element_type=jnp.float32
            ).astype(jnp.bfloat16)
            for n, target in enumerate(targets):
                for k in range(4):
                    target[lax.div(c, 2), lax.rem(c, 2) * 4 + k] = part[
                        n * HEAD : (n + 1) * HEAD, k * ROWS : (k + 1) * ROWS
                    ]
            return carry

        lax.fori_loop(0, FEATURES // 512, step, 0)

    kv_copy = remote(dwo, kv_near, kv_sem.at[0], kv_sem.at[1], me.to("core"))

    def f_copy(source, kind, j):
        to = lax.rem(me.z + j, 8)
        return remote(
            source.at[:, to], f_in.at[kind, j], f_send.at[kind, j], f_recv.at[kind, j], (me.lo * 8 + to, me.s)
        )

    def f_start(source, kind):
        def step(j, carry):
            f_copy(source, kind, j).start()
            return carry

        lax.fori_loop(1, 8, step, 0)

    def lo_copy(kind):
        return remote(lo_out.at[kind], lo_in.at[kind], f_send.at[kind, 0], f_recv.at[kind, 0], me.to("lo"))

    def f_sum(source, kind):
        def step(j, totals):
            f_copy(source, kind, j).wait()
            return (
                totals[0] + f_in[kind, j, me.lo].astype(jnp.float32),
                totals[1] + f_in[kind, j, 1 - me.lo].astype(jnp.float32),
            )

        own, other = lax.fori_loop(
            1,
            8,
            step,
            (source[me.lo, me.z].astype(jnp.float32), source[1 - me.lo, me.z].astype(jnp.float32)),
        )
        lo_out[kind] = other.astype(jnp.bfloat16)
        lo_copy(kind).start()
        return own

    def f_total(own, kind):
        lo_copy(kind).wait()
        return own + lo_in[kind].astype(jnp.float32)

    chip = lax.div(me.s, 2)

    def a_copy(j, source):
        slot = kv_all.at[me.core, source]
        to = (me.f, lax.rem(me.s + 2 * j, N_SEQ))
        return remote(slot, slot, a_send.at[j], a_recv.at[j], to)

    def a_start(j, carry):
        a_copy(j, chip).start()
        return carry

    def a_arrived(j, carry):
        a_copy(j, lax.rem(chip + 8 - j, 8)).wait_recv()
        return carry

    def a_sent(j, carry):
        a_copy(j, chip).wait_send()
        return carry

    def r_start(*pieces):
        for i in pieces:
            r_copy(i).start()

    block_out((2, 1))
    block_out((-1, 1))
    block_in((2, 1))
    r_start(0, 1, 2)
    block_out((1, 1))
    block_in((-1, 1))
    r_start(3, 5)
    block_in((1, 1))
    r_start(4, 6)
    weights(HEAD, 2 * HEAD, (dwm, dwo))
    kv_copy.start()
    block_out((2, 0))
    r_add(0)
    r_start(7)
    r_add(1)
    r_start(8)
    kv_copy.wait_recv()

    def kv_add(z, carry):
        for lo in (0, 1):
            dwm[lo, z] = (dwm[lo, z].astype(jnp.float32) + kv_near[lo, z].astype(jnp.float32)).astype(
                jnp.bfloat16
            )
        return carry

    lax.fori_loop(0, 8, kv_add, 0)
    f_start(dwm, 1)
    block_in((2, 0))
    r_add(2)
    r_start(9, 10)
    block_out((-1, 0))
    block_out((1, 0))
    block_in((-1, 0))
    r_start(11)
    block_in((1, 0))
    r_start(12)
    weights(0, HEAD, (dwq,))
    f_start(dwq, 0)
    block_out((0, 1))
    block_out((0, 0))
    block_in((0, 1))
    r_add(3)
    r_add(4)
    r_start(13, 14)
    block_in((0, 0))
    r_add(5)
    r_add(7)
    r_add(6)
    r_add(8)
    r_add(9)
    r_start(15)
    r_add(10)
    r_start(16)
    kv_own = f_sum(dwm, 1)
    kv_all[me.core, chip] = f_total(kv_own, 1).astype(jnp.bfloat16)
    lax.fori_loop(1, 8, a_start, 0)
    q_own = f_sum(dwq, 0)
    lax.fori_loop(1, 8, a_arrived, 0)
    kv_mine, kv_theirs = kv_all.at[me.core], kv_all.at[1 - me.core]
    kv_share = remote(kv_mine, kv_mine, kv_sem.at[2], kv_sem.at[3], me.to("core"))
    kv_share.start()
    for first, pieces in LAST:
        total = mine[SLOT[(0, 0)], pl.ds(first, 64), :].astype(jnp.float32)
        for i in pieces:
            r_copy(i).wait_recv()
            total = total + arrived[pl.ds(RECV_AT[i], 64), :].astype(jnp.float32)
        in_ref[pl.ds(first, 64), :] = total.astype(jnp.bfloat16)
    dq_ref[...] = f_total(q_own, 0).T
    remote(kv_theirs, kv_theirs, kv_sem.at[2], kv_sem.at[3], me.to("core")).wait_recv()
    for n in range(4):
        at = pl.ds(n * HEAD, HEAD)
        for kind, out in ((0, dk_ref), (1, dv_ref)):
            out[:, at] = (
                kv_all[kind, 2 * n].astype(jnp.float32) + kv_all[kind, 2 * n + 1].astype(jnp.float32)
            ).T
    lax.fori_loop(1, 8, a_sent, 0)
    kv_share.wait_send()
    kv_copy.wait_send()
    for i in range(len(REDUCE)):
        r_copy(i).wait_send()
    for n in range(len(ORDER)):
        near_copy(n).wait_send()


def whole_kernel(
    x_hbm, g_hbm, wq_hbm, wk_hbm, wv_hbm, cos_hbm, sin_hbm, b_ref,
    in_ref, dq_ref, dk_ref, dv_ref,
    rows, q_ref, k_ref, v_ref, grad_ref, w_ref, cos_ref, sin_ref,
    sc, dp_sc, dk_sc, dv_sc, kt_sc, cols,
    mine, away, near, arrived, dwq, dwm, dwo, kv_near, f_in, lo_out, lo_in, kv_all,
    *sems,
):
    me = Place()
    gather(
        me, x_hbm, g_hbm, wq_hbm, wk_hbm, wv_hbm, cos_hbm, sin_hbm,
        rows, q_ref, k_ref, v_ref, grad_ref, w_ref, cos_ref, sin_ref, *sems[:9],
    )
    attention(me, b_ref, q_ref, k_ref, v_ref, grad_ref, cos_ref, sin_ref, cols, sc, dp_sc, dk_sc, dv_sc, kt_sc)
    scatter(
        me, cols, w_ref, rows, in_ref, dq_ref, dk_ref, dv_ref,
        mine, away, near, arrived, dwq, dwm, dwo, kv_near, f_in, lo_out, lo_in, kv_all, *sems[9:],
    )


def rope_tables():
    half = HEAD // 2
    inverse = (500000.0 ** (-(np.arange(half, dtype=np.float64) * 2.0 / HEAD))).astype(np.float32)
    angles = np.arange(LENGTH, dtype=np.float32)[:, None] * inverse[None, :]
    cos, sin = np.cos(angles), np.sin(angles)
    return np.concatenate([cos, cos], axis=1), np.concatenate([-sin, sin], axis=1)


def vmem():
    return pl.BlockSpec(memory_space=pltpu.VMEM)


BF16, F32 = jnp.bfloat16, jnp.float32
dma = pltpu.SemaphoreType.DMA
shape = jax.ShapeDtypeStruct
VMEM_LIMIT = 62 * 2**20


def run(x, g, wq, wk, wv, cos, sin, boundary):
    per_head = pltpu.VMEM((LENGTH, HEAD), BF16)
    table = pltpu.VMEM((LENGTH, HEAD), F32)
    scores = pltpu.VMEM((LENGTH, QB), F32)
    blocks = pltpu.VMEM((8, ROWS, FEATURES), BF16)
    pieces = pltpu.VMEM((2, 8, HEAD, ROWS), BF16)
    pair = pltpu.VMEM((2, HEAD, ROWS), BF16)
    hbm = pl.BlockSpec(memory_space=pltpu.HBM)
    return pl.pallas_call(
        whole_kernel,
        out_shape=(
            shape((ROWS, FEATURES), BF16),
            shape((ROWS, HEAD), F32),
            shape((ROWS, GROUP * HEAD), F32),
            shape((ROWS, GROUP * HEAD), F32),
        ),
        in_specs=[hbm] * 7 + [pl.BlockSpec(memory_space=pltpu.SMEM)],
        out_specs=(vmem(),) * 4,
        scratch_shapes=[
            pltpu.VMEM((LENGTH, FEATURES), BF16),
            per_head,
            per_head,
            per_head,
            per_head,
            pltpu.VMEM((FEATURES, 3 * HEAD), BF16),
            table,
            table,
            scores,
            scores,
            table,
            table,
            pltpu.VMEM((HEAD, LENGTH), BF16),
            pltpu.VMEM((LENGTH, 3 * HEAD), BF16),
            blocks,
            blocks,
            blocks,
            pltpu.VMEM((RECV_ROWS, FEATURES), BF16),
            pieces,
            pieces,
            pieces,
            pieces,
            pltpu.VMEM((2, 8, 2, HEAD, ROWS), BF16),
            pair,
            pair,
            pltpu.VMEM((2, 8, HEAD, ROWS), BF16),
            dma((len(GATHER),)),
            dma((len(GATHER),)),
            dma((len(GATHER) + 1,)),
            dma((len(GATHER) + 1,)),
            dma((N_SEQ,)),
            dma((N_SEQ,)),
            dma((18,)),
            dma((18,)),
            dma((6,)),
            dma((len(REDUCE),)),
            dma((len(REDUCE),)),
            dma((len(ORDER),)),
            dma((len(ORDER),)),
            dma((4,)),
            dma((2, 8)),
            dma((2, 8)),
            dma((8,)),
            dma((8,)),
        ],
        compiler_params=pltpu.CompilerParams(collective_id=1, has_side_effects=True, vmem_limit_bytes=VMEM_LIMIT),
        name="attention_backward",
    )(x, g, wq, wk, wv, cos, sin, boundary)


def copy_kernel(*refs):
    ins, outs, sem = refs[:4], refs[4:8], refs[8]
    copies = [pltpu.make_async_copy(a, b, sem.at[n]) for n, (a, b) in enumerate(zip(ins, outs))]
    for copy in copies:
        copy.start()
    for copy in copies:
        copy.wait()


def place_outputs(*arrays):
    hbm = pl.BlockSpec(memory_space=pltpu.HBM)
    return pl.pallas_call(
        copy_kernel,
        out_shape=tuple(shape(a.shape, a.dtype) for a in arrays),
        in_specs=[hbm] * 4,
        out_specs=(hbm,) * 4,
        scratch_shapes=[dma((4,))],
        compiler_params=pltpu.CompilerParams(vmem_limit_bytes=VMEM_LIMIT),
        name="place_outputs",
    )(*arrays)


def shards(normed_input, out_grad, w_query, key_weight_matrix, value_weight_matrix, boundary):
    cos, sin = rope_tables()
    input_grad, dq, dk, dv = run(
        normed_input[0], out_grad[0], w_query, key_weight_matrix, value_weight_matrix,
        jnp.asarray(cos), jnp.asarray(sin), boundary,
    )
    input_grad, dq, dk, dv = place_outputs(input_grad, dq, dk, dv)
    return (input_grad[None], dq, dk, dv)


def solution(mesh):
    return jax.shard_map(
        shards,
        mesh=mesh,
        in_specs=(
            P("fsdp", "seq", None),
            P("fsdp", "seq", None),
            P("fsdp", "seq"),
            P("fsdp", None),
            P("fsdp", None),
            P("fsdp"),
        ),
        out_specs=(P("fsdp", "seq", None), P("fsdp", "seq"), P("fsdp", None), P("fsdp", None)),
        check_vma=False,
    )
```

```python
import jax
import jax.numpy as jnp
import numpy as np
from jax import lax
from jax.experimental import pallas as pl
from jax.experimental.pallas import tpu as pltpu
from jax.sharding import PartitionSpec as P

HEAD = 128
N_SEQ = 16
N_FSDP = 16
ROWS = 128
LENGTH = 2048
FEATURES = 2048
GROUP = 4
MESH = pl.DeviceIdType.MESH
SCALE = HEAD ** (-0.5)
EXP2_SCALE = SCALE * 1.4426950408889634

GATHER = (
    ("up", (0, 0), 0, 64, (-1, 0)),
    ("down", (0, 0), 64, 64, (1, 0)),
    ("side", (0, 0), 0, 64, (0, 1)),
    ("up", (0, 0), 64, 64, (-1, 0)),
    ("down", (0, 0), 0, 64, (1, 0)),
    ("side", (0, 0), 64, 64, (0, 1)),
    ("up", (-1, 0), 0, 64, (2, 0)),
    ("down", (1, 0), 64, 64, (2, 0)),
    ("side", (-1, 0), 0, 48, (-1, 1)),
    ("side", (1, 0), 80, 48, (1, 1)),
    ("down", (0, 1), 0, 64, (1, 1)),
    ("up", (0, 1), 64, 64, (-1, 1)),
    ("up", (-1, 1), 0, 48, (2, 1)),
    ("down", (1, 1), 80, 48, (2, 1)),
    ("side", (2, 0), 48, 32, (2, 1)),
    ("side", (-1, 0), 48, 16, (-1, 1)),
    ("side", (1, 0), 64, 16, (1, 1)),
)

REDUCE = (
    ("down", (2, 1), 0, 48, (-1, 1)),
    ("up", (2, 1), 80, 48, (1, 1)),
    ("side", (2, 1), 48, 32, (2, 0)),
    ("down", (-1, 1), 64, 64, (0, 1)),
    ("up", (1, 1), 0, 64, (0, 1)),
    ("side", (-1, 1), 48, 16, (-1, 0)),
    ("side", (1, 1), 64, 16, (1, 0)),
    ("side", (-1, 1), 0, 48, (-1, 0)),
    ("side", (1, 1), 80, 48, (1, 0)),
    ("down", (2, 0), 0, 64, (-1, 0)),
    ("up", (2, 0), 64, 64, (1, 0)),
    ("down", (-1, 0), 64, 64, (0, 0)),
    ("up", (1, 0), 0, 64, (0, 0)),
    ("side", (0, 1), 0, 64, (0, 0)),
    ("side", (0, 1), 64, 64, (0, 0)),
    ("down", (-1, 0), 0, 64, (0, 0)),
    ("up", (1, 0), 64, 64, (0, 0)),
)
LAST = ((0, (12, 13, 15)), (64, (11, 14, 16)))


class Place:
    def __init__(self):
        self.f = lax.axis_index("fsdp")
        self.s = lax.axis_index("seq")
        self.core = lax.rem(self.s, 2)
        self.hi = lax.rem(lax.div(self.s, 2), 2)
        self.y = lax.div(self.s, 4)
        self.z = lax.rem(self.f, 8)
        self.lo = lax.div(self.f, 8)

    def to(self, direction):
        s = self.s
        if direction == "up":
            return (self.f, lax.rem(s + 4, N_SEQ))
        if direction == "down":
            return (self.f, lax.rem(s + 12, N_SEQ))
        if direction == "side":
            return (self.f, s + 2 - 4 * self.hi)
        if direction == "lo":
            return ((1 - self.lo) * 8 + self.z, s)
        return (self.f, s + 1 - 2 * self.core)

    def block(self, rel, other_core=0):
        dy, dh = rel
        y = lax.rem(self.y + dy + 4, 4)
        hi = 1 - self.hi if dh else self.hi
        core = 1 - self.core if other_core else self.core
        return y * 4 + hi * 2 + core


def enter(me):
    barrier = pltpu.get_barrier_semaphore()

    def greet(device):
        pl.semaphore_signal(barrier, inc=1, device_id=device, device_id_type=MESH)

    def greet_seq(j, carry):
        greet((me.f, lax.rem(me.s + j, N_SEQ)))
        return carry

    def greet_z(j, carry):
        greet((me.lo * 8 + lax.rem(me.z + j, 8), me.s))
        return carry

    lax.fori_loop(1, N_SEQ, greet_seq, 0)
    lax.fori_loop(1, 8, greet_z, 0)
    greet(me.to("lo"))
    pl.semaphore_wait(barrier, N_SEQ - 1 + 8)


def remote(src, dst, send, recv, device):
    return pltpu.make_async_remote_copy(
        src_ref=src,
        dst_ref=dst,
        send_sem=send,
        recv_sem=recv,
        device_id=device,
        device_id_type=MESH,
    )


CHIP_PARTS = (
    ((-1, 0), (0, 3)),
    ((1, 0), (1, 4)),
    ((0, 1), (2, 5)),
    ((2, 0), (6, 7)),
    ((-1, 1), (8, 11, 15)),
    ((1, 1), (9, 10, 16)),
    ((2, 1), (12, 13, 14)),
)


def gather(
    me, x_hbm, g_hbm, wq_hbm, wk_hbm, wv_hbm, cos_hbm, sin_hbm,
    rows, q_ref, k_ref, v_ref, grad_ref, w_ref,
    cos_ref, sin_ref, x_send, x_recv, c_send, c_recv, g_send, g_recv, w_send, w_recv, l_sem,
):
    own = pl.multiple_of(me.s * ROWS, ROWS)
    head_col = pl.multiple_of(me.y * HEAD, HEAD)
    own_w = pl.ds(pl.multiple_of(me.f * ROWS, ROWS), ROWS)
    loads = [
        pltpu.make_async_copy(wq_hbm, w_ref.at[own_w, pl.ds(0, HEAD)], l_sem.at[0]),
        pltpu.make_async_copy(wk_hbm.at[:, pl.ds(head_col, HEAD)], w_ref.at[own_w, pl.ds(HEAD, HEAD)], l_sem.at[1]),
        pltpu.make_async_copy(wv_hbm.at[:, pl.ds(head_col, HEAD)], w_ref.at[own_w, pl.ds(HEAD, HEAD)], l_sem.at[1]),
        pltpu.make_async_copy(x_hbm, rows.at[pl.ds(own, ROWS), :], l_sem.at[2]),
        pltpu.make_async_copy(cos_hbm, cos_ref, l_sem.at[3]),
        pltpu.make_async_copy(sin_hbm, sin_ref, l_sem.at[4]),
        pltpu.make_async_copy(g_hbm.at[:, pl.ds(own, HEAD)], grad_ref.at[pl.ds(own, ROWS), :], l_sem.at[5]),
    ]
    loads[0].start()

    @pl.when(me.core == 0)
    def _():
        loads[1].start()

    @pl.when(me.core == 1)
    def _():
        loads[2].start()

    for load in loads[3:]:
        load.start()

    enter(me)

    def w_piece(lo, z):
        at = pl.multiple_of((lo * 8 + z) * ROWS, ROWS)
        return w_ref.at[pl.ds(at, ROWS), pl.ds(0, 2 * HEAD)]

    def w_copy(lo, z, slot, device):
        piece = w_piece(lo, z)
        return remote(piece, piece, w_send.at[slot], w_recv.at[slot], device)

    def along(dz):
        return (me.lo * 8 + lax.rem(me.z + dz + 8, 8), me.s)

    def w_move(other, held, hop):
        lo = 1 - me.lo if other else me.lo
        return w_copy(lo, lax.rem(me.z + held + 8, 8), 9 * other + 4 + hop - held, along(hop))

    def w_arrival(other, away):
        lo = 1 - me.lo if other else me.lo
        return w_copy(lo, lax.rem(me.z + away + 8, 8), 9 * other + 4 - away, along(1))

    first_moves = [(0, hop) for hop in (1, -1, 2, -2)]
    next_moves = {0: ((-2, 1), (2, -1), (-2, 2)), 1: ((-2, 1), (2, -1), (2, -2))}

    def w_start(other):
        for held, hop in first_moves:
            w_move(other, held, hop).start()

    def w_onward(other):
        w_arrival(other, -2).wait_recv()
        w_arrival(other, 2).wait_recv()
        for held, hop in next_moves[other]:
            w_move(other, held, hop).start()

    def w_finish():
        for other in (0, 1):
            for away in (-1, 1, -3, 3, -4 if other == 0 else 4):
                w_arrival(other, away).wait_recv()

    def w_sent():
        for other in (0, 1):
            for held, hop in first_moves + list(next_moves[other]):
                w_move(other, held, hop).wait_send()

    def part(rel, first, count, other_core=0):
        at = pl.multiple_of(me.block(rel, other_core) * ROWS + first, 16)
        return rows.at[pl.ds(at, count), :]

    def x_copy(i):
        direction, rel, first, count, _ = GATHER[i]
        piece = part(rel, first, count)
        source = x_hbm.at[pl.ds(first, count), :] if rel == (0, 0) else piece
        return remote(source, piece, x_send.at[i], x_recv.at[i], me.to(direction))

    def x_start(i):
        x_copy(i).start()

    def x_arrived(i):
        direction, _, first, count, rel = GATHER[i]
        piece = part(rel, first, count)
        remote(piece, piece, x_send.at[i], x_recv.at[i], me.to(direction)).wait_recv()
        core_copy(i).start()

    def core_copy(i, receive=False):
        rel, first, count = (0, 0), 0, 128
        if i < len(GATHER):
            _, _, first, count, rel = GATHER[i]
        piece = part(rel, first, count, other_core=1 if receive else 0)
        source = x_hbm if rel == (0, 0) and not receive else piece
        return remote(source, piece, c_send.at[i], c_recv.at[i], me.to("core"))

    def g_copy(j, device_s, source_s):
        at = pl.multiple_of(source_s * ROWS, ROWS)
        col = pl.multiple_of(device_s * HEAD, HEAD)
        return remote(
            g_hbm.at[:, pl.ds(col, HEAD)],
            grad_ref.at[pl.ds(at, ROWS), :],
            g_send.at[j],
            g_recv.at[j],
            (me.f, device_s),
        )

    def g_start(j, carry):
        g_copy(j, lax.rem(me.s + j, N_SEQ), me.s).start()
        return carry

    def project(rel, parts):
        for i in parts:
            core_copy(i, True).wait_recv()
        hi = 1 - me.hi if rel[1] else me.hi
        chip = lax.rem(me.y + rel[0] + 4, 4) * 2 + hi
        at = pl.ds(pl.multiple_of(chip * 256, 256), 256)
        full = jnp.dot(rows[at, :], w_ref[...], preferred_element_type=jnp.float32)
        cos, sin = cos_ref[at, :], sin_ref[at, :]
        q, first, second = full[:, :HEAD], full[:, HEAD : 2 * HEAD], full[:, 2 * HEAD :]
        is_key = me.core == 0
        k, v = jnp.where(is_key, first, second), jnp.where(is_key, second, first)
        q_ref[at, :] = (q * cos + pltpu.roll(q, HEAD // 2, 1) * sin).astype(jnp.bfloat16)
        k_ref[at, :] = (k * cos + pltpu.roll(k, HEAD // 2, 1) * sin).astype(jnp.bfloat16)
        v_ref[at, :] = v.astype(jnp.bfloat16)

    for i in range(6):
        x_start(i)
    loads[0].wait()
    loads[1].wait()
    own_to_lo = w_copy(me.lo, me.z, 4, me.to("lo"))
    own_to_lo.start()
    w_start(0)
    core_copy(len(GATHER)).start()
    w_copy(1 - me.lo, me.z, 4, me.to("lo")).wait_recv()
    w_start(1)
    x_arrived(0)
    x_start(6)
    x_start(8)
    x_arrived(1)
    x_start(7)
    x_start(9)
    x_start(15)
    x_start(16)
    x_arrived(2)
    x_start(10)
    w_onward(0)
    w_onward(1)
    x_arrived(5)
    x_start(11)
    x_arrived(3)
    x_arrived(4)
    x_arrived(8)
    x_start(12)
    x_arrived(9)
    x_start(13)
    x_arrived(6)
    x_arrived(7)
    x_start(14)
    lax.fori_loop(1, N_SEQ, g_start, 0)
    for load in loads[3:]:
        load.wait()
    w_finish()
    share = remote(
        w_ref.at[:, pl.ds(HEAD, HEAD)],
        w_ref.at[:, pl.ds(2 * HEAD, HEAD)],
        w_send.at[17],
        w_recv.at[17],
        me.to("core"),
    )
    share.start()
    share.wait_recv()
    project((0, 0), (len(GATHER),))
    for rel, parts in CHIP_PARTS[:4]:
        project(rel, parts)
    x_arrived(10)
    x_arrived(11)
    x_arrived(15)
    x_arrived(16)
    for rel, parts in CHIP_PARTS[4:6]:
        project(rel, parts)
    for i in CHIP_PARTS[6][1]:
        x_arrived(i)
    project(*CHIP_PARTS[6])

    def g_finish(j, carry):
        back = lax.rem(me.s + N_SEQ - j, N_SEQ)
        g_copy(j, back, back).wait_recv()
        g_copy(j, lax.rem(me.s + j, N_SEQ), me.s).wait_send()
        return carry

    lax.fori_loop(1, N_SEQ, g_finish, 0)
    share.wait_send()
    own_to_lo.wait_send()
    w_sent()
    for i in range(len(GATHER)):
        x_copy(i).wait_send()
    for i in range(len(GATHER) + 1):
        core_copy(i).wait_send()


NT = (((1,), (1,)), ((), ()))
TN = (((0,), (0,)), ((), ()))
QB = 256


def attention(me, b_ref, q_ref, k_ref, v_ref, g_ref, cos_ref, sin_ref, out_ref, sc, dp_sc, dk_sc, dv_sc, kt_sc):
    start = b_ref[0]
    kt_sc[...] = k_ref[...].T
    for i in range(LENGTH // QB):
        rows_i = pl.ds(i * QB, QB)
        q = q_ref[rows_i, :]
        g = g_ref[rows_i, :]
        q_pos = i * QB + lax.broadcasted_iota(jnp.int32, (1, QB), 1)
        low = jnp.where(q_pos < start, 0, start)
        top = jnp.full((1, QB), -1e30, jnp.float32)
        for j in range(i + 1):
            at = pl.ds(j * QB, QB)
            s = lax.dot_general(k_ref[at, :], q, NT, preferred_element_type=jnp.float32)
            k_pos = j * QB + lax.broadcasted_iota(jnp.int32, (QB, QB), 0)
            ok = k_pos >= low
            if j == i:
                ok = ok & (k_pos <= q_pos)
            s = jnp.where(ok, s, -1e30)
            sc[at, :] = s
            top = jnp.maximum(top, jnp.max(s, axis=0, keepdims=True))
        top = top * EXP2_SCALE
        total = jnp.zeros((1, QB), jnp.float32)
        for j in range(i + 1):
            at = pl.ds(j * QB, QB)
            e = jnp.exp2(sc[at, :] * EXP2_SCALE - top)
            sc[at, :] = e
            total = total + jnp.sum(e, axis=0, keepdims=True)
        inverse = 1.0 / total
        delta = jnp.zeros((1, QB), jnp.float32)
        for j in range(i + 1):
            at = pl.ds(j * QB, QB)
            p = sc[at, :] * inverse
            sc[at, :] = p
            low_p = p.astype(jnp.bfloat16)
            d = lax.dot_general(v_ref[at, :], g, NT, preferred_element_type=jnp.float32)
            dp_sc[at, :] = d
            delta = delta + jnp.sum(low_p.astype(jnp.float32) * d, axis=0, keepdims=True)
            dv = jnp.dot(low_p, g, preferred_element_type=jnp.float32)
            if j == i:
                dv_sc[at, :] = dv
            else:
                dv_sc[at, :] += dv
        dq = jnp.zeros((HEAD, QB), jnp.float32)
        for j in range(i + 1):
            at = pl.ds(j * QB, QB)
            ds = (sc[at, :] * (dp_sc[at, :] - delta)).astype(jnp.bfloat16)
            dk = jnp.dot(ds, q, preferred_element_type=jnp.float32)
            if j == i:
                dk_sc[at, :] = dk
            else:
                dk_sc[at, :] += dk
            dq = dq + jnp.dot(kt_sc[:, at], ds, preferred_element_type=jnp.float32)
        dq = dq.T * SCALE
        out_ref[rows_i, :HEAD] = (
            dq * cos_ref[rows_i, :] - pltpu.roll(dq, HEAD // 2, 1) * sin_ref[rows_i, :]
        ).astype(jnp.bfloat16)

    key_col = pl.ds(pl.multiple_of(HEAD + me.core * HEAD, HEAD), HEAD)
    value_col = pl.ds(pl.multiple_of(2 * HEAD - me.core * HEAD, HEAD), HEAD)

    def finish(c, carry):
        at = pl.ds(pl.multiple_of(c * QB, QB), QB)
        dk = dk_sc[at, :] * SCALE
        out_ref[at, key_col] = (
            dk * cos_ref[at, :] - pltpu.roll(dk, HEAD // 2, 1) * sin_ref[at, :]
        ).astype(jnp.bfloat16)
        out_ref[at, value_col] = dv_sc[at, :].astype(jnp.bfloat16)
        return carry

    lax.fori_loop(0, LENGTH // QB, finish, 0)


ORDER = ((2, 1), (-1, 1), (1, 1), (2, 0), (0, 1), (-1, 0), (1, 0), (0, 0))
SLOT = {rel: n for n, rel in enumerate(ORDER)}
RECV_AT = []
_at = 0
for _piece in REDUCE:
    RECV_AT.append(_at)
    _at += _piece[3]
RECV_ROWS = _at


def scatter(
    me, g_ref, w_ref, rows, in_ref, dq_ref, dk_ref, dv_ref,
    mine, away, near, arrived, dwq, dwm, dwo, kv_near, f_in, lo_out, lo_in, kv_all,
    r_send, r_recv, n_send, n_recv, kv_sem, f_send, f_recv, a_send, a_recv,
):
    def partial_sum(rel, other_core):
        at = pl.ds(pl.multiple_of(me.block(rel, other_core) * ROWS, ROWS), ROWS)
        return lax.dot_general(
            g_ref[at, :], w_ref[...], NT, preferred_element_type=jnp.float32
        ).astype(jnp.bfloat16)

    def near_copy(n):
        return remote(away.at[n], near.at[n], n_send.at[n], n_recv.at[n], me.to("core"))

    def block_out(rel):
        n = SLOT[rel]
        away[n] = partial_sum(rel, 1)
        near_copy(n).start()
        mine[n] = partial_sum(rel, 0)

    def block_in(rel):
        n = SLOT[rel]
        near_copy(n).wait_recv()
        mine[n] = (mine[n].astype(jnp.float32) + near[n].astype(jnp.float32)).astype(jnp.bfloat16)

    def r_copy(i):
        direction, rel, first, count, _ = REDUCE[i]
        return remote(
            mine.at[SLOT[rel], pl.ds(first, count), :],
            arrived.at[pl.ds(RECV_AT[i], count), :],
            r_send.at[i],
            r_recv.at[i],
            me.to(direction),
        )

    def r_add(i):
        _, _, first, count, rel = REDUCE[i]
        r_copy(i).wait_recv()
        n = SLOT[rel]
        mine[n, pl.ds(first, count), :] = (
            mine[n, pl.ds(first, count), :].astype(jnp.float32)
            + arrived[pl.ds(RECV_AT[i], count), :].astype(jnp.float32)
        ).astype(jnp.bfloat16)

    def weights(first_col, count, targets):
        def step(c, carry):
            at = pl.ds(pl.multiple_of(c * 512, 512), 512)
            part = lax.dot_general(
                g_ref[:, pl.ds(first_col, count)], rows[:, at], TN, preferred_element_type=jnp.float32
            ).astype(jnp.bfloat16)
            for n, target in enumerate(targets):
                for k in range(4):
                    target[lax.div(c, 2), lax.rem(c, 2) * 4 + k] = part[
                        n * HEAD : (n + 1) * HEAD, k * ROWS : (k + 1) * ROWS
                    ]
            return carry

        lax.fori_loop(0, FEATURES // 512, step, 0)

    kv_copy = remote(dwo, kv_near, kv_sem.at[0], kv_sem.at[1], me.to("core"))

    def f_copy(source, kind, j):
        to = lax.rem(me.z + j, 8)
        return remote(
            source.at[:, to], f_in.at[kind, j], f_send.at[kind, j], f_recv.at[kind, j], (me.lo * 8 + to, me.s)
        )

    def f_start(source, kind):
        def step(j, carry):
            f_copy(source, kind, j).start()
            return carry

        lax.fori_loop(1, 8, step, 0)

    def lo_copy(kind):
        return remote(lo_out.at[kind], lo_in.at[kind], f_send.at[kind, 0], f_recv.at[kind, 0], me.to("lo"))

    def f_sum(source, kind):
        def step(j, totals):
            f_copy(source, kind, j).wait()
            return (
                totals[0] + f_in[kind, j, me.lo].astype(jnp.float32),
                totals[1] + f_in[kind, j, 1 - me.lo].astype(jnp.float32),
            )

        own, other = lax.fori_loop(
            1,
            8,
            step,
            (source[me.lo, me.z].astype(jnp.float32), source[1 - me.lo, me.z].astype(jnp.float32)),
        )
        lo_out[kind] = other.astype(jnp.bfloat16)
        lo_copy(kind).start()
        return own

    def f_total(own, kind):
        lo_copy(kind).wait()
        return own + lo_in[kind].astype(jnp.float32)

    chip = lax.div(me.s, 2)

    def a_copy(j, source):
        slot = kv_all.at[me.core, source]
        to = (me.f, lax.rem(me.s + 2 * j, N_SEQ))
        return remote(slot, slot, a_send.at[j], a_recv.at[j], to)

    def a_start(j, carry):
        a_copy(j, chip).start()
        return carry

    def a_arrived(j, carry):
        a_copy(j, lax.rem(chip + 8 - j, 8)).wait_recv()
        return carry

    def a_sent(j, carry):
        a_copy(j, chip).wait_send()
        return carry

    def r_start(*pieces):
        for i in pieces:
            r_copy(i).start()

    block_out((2, 1))
    block_out((-1, 1))
    block_in((2, 1))
    r_start(0, 1, 2)
    block_out((1, 1))
    block_in((-1, 1))
    r_start(3, 5)
    block_in((1, 1))
    r_start(4, 6)
    weights(HEAD, 2 * HEAD, (dwm, dwo))
    kv_copy.start()
    block_out((2, 0))
    r_add(0)
    r_start(7)
    r_add(1)
    r_start(8)
    kv_copy.wait_recv()

    def kv_add(z, carry):
        for lo in (0, 1):
            dwm[lo, z] = (dwm[lo, z].astype(jnp.float32) + kv_near[lo, z].astype(jnp.float32)).astype(
                jnp.bfloat16
            )
        return carry

    lax.fori_loop(0, 8, kv_add, 0)
    f_start(dwm, 1)
    block_in((2, 0))
    r_add(2)
    r_start(9, 10)
    block_out((-1, 0))
    block_out((1, 0))
    block_in((-1, 0))
    r_start(11)
    block_in((1, 0))
    r_start(12)
    weights(0, HEAD, (dwq,))
    f_start(dwq, 0)
    block_out((0, 1))
    block_out((0, 0))
    block_in((0, 1))
    r_add(3)
    r_add(4)
    r_start(13, 14)
    block_in((0, 0))
    r_add(5)
    r_add(7)
    r_add(6)
    r_add(8)
    r_add(9)
    r_start(15)
    r_add(10)
    r_start(16)
    kv_own = f_sum(dwm, 1)
    kv_all[me.core, chip] = f_total(kv_own, 1).astype(jnp.bfloat16)
    lax.fori_loop(1, 8, a_start, 0)
    q_own = f_sum(dwq, 0)
    lax.fori_loop(1, 8, a_arrived, 0)
    kv_mine, kv_theirs = kv_all.at[me.core], kv_all.at[1 - me.core]
    kv_share = remote(kv_mine, kv_mine, kv_sem.at[2], kv_sem.at[3], me.to("core"))
    kv_share.start()
    for first, pieces in LAST:
        total = mine[SLOT[(0, 0)], pl.ds(first, 64), :].astype(jnp.float32)
        for i in pieces:
            r_copy(i).wait_recv()
            total = total + arrived[pl.ds(RECV_AT[i], 64), :].astype(jnp.float32)
        in_ref[pl.ds(first, 64), :] = total.astype(jnp.bfloat16)
    dq_ref[...] = f_total(q_own, 0).T
    remote(kv_theirs, kv_theirs, kv_sem.at[2], kv_sem.at[3], me.to("core")).wait_recv()
    for n in range(4):
        at = pl.ds(n * HEAD, HEAD)
        for kind, out in ((0, dk_ref), (1, dv_ref)):
            out[:, at] = (
                kv_all[kind, 2 * n].astype(jnp.float32) + kv_all[kind, 2 * n + 1].astype(jnp.float32)
            ).T
    lax.fori_loop(1, 8, a_sent, 0)
    kv_share.wait_send()
    kv_copy.wait_send()
    for i in range(len(REDUCE)):
        r_copy(i).wait_send()
    for n in range(len(ORDER)):
        near_copy(n).wait_send()


def whole_kernel(
    x_hbm, g_hbm, wq_hbm, wk_hbm, wv_hbm, cos_hbm, sin_hbm, b_ref,
    in_ref, dq_ref, dk_ref, dv_ref,
    rows, q_ref, k_ref, v_ref, grad_ref, w_ref, cos_ref, sin_ref,
    sc, dp_sc, dk_sc, dv_sc, kt_sc, cols,
    mine, away, near, arrived, dwq, dwm, dwo, kv_near, f_in, lo_out, lo_in, kv_all,
    *sems,
):
    me = Place()
    gather(
        me, x_hbm, g_hbm, wq_hbm, wk_hbm, wv_hbm, cos_hbm, sin_hbm,
        rows, q_ref, k_ref, v_ref, grad_ref, w_ref, cos_ref, sin_ref, *sems[:9],
    )
    attention(me, b_ref, q_ref, k_ref, v_ref, grad_ref, cos_ref, sin_ref, cols, sc, dp_sc, dk_sc, dv_sc, kt_sc)
    scatter(
        me, cols, w_ref, rows, in_ref, dq_ref, dk_ref, dv_ref,
        mine, away, near, arrived, dwq, dwm, dwo, kv_near, f_in, lo_out, lo_in, kv_all, *sems[9:],
    )


def rope_tables():
    half = HEAD // 2
    inverse = (500000.0 ** (-(np.arange(half, dtype=np.float64) * 2.0 / HEAD))).astype(np.float32)
    angles = np.arange(LENGTH, dtype=np.float32)[:, None] * inverse[None, :]
    cos, sin = np.cos(angles), np.sin(angles)
    return np.concatenate([cos, cos], axis=1), np.concatenate([-sin, sin], axis=1)


def vmem():
    return pl.BlockSpec(memory_space=pltpu.VMEM)


BF16, F32 = jnp.bfloat16, jnp.float32
dma = pltpu.SemaphoreType.DMA
shape = jax.ShapeDtypeStruct
VMEM_LIMIT = 62 * 2**20


def run(x, g, wq, wk, wv, cos, sin, boundary):
    per_head = pltpu.VMEM((LENGTH, HEAD), BF16)
    table = pltpu.VMEM((LENGTH, HEAD), F32)
    scores = pltpu.VMEM((LENGTH, QB), F32)
    blocks = pltpu.VMEM((8, ROWS, FEATURES), BF16)
    pieces = pltpu.VMEM((2, 8, HEAD, ROWS), BF16)
    pair = pltpu.VMEM((2, HEAD, ROWS), BF16)
    hbm = pl.BlockSpec(memory_space=pltpu.HBM)
    return pl.pallas_call(
        whole_kernel,
        out_shape=(
            shape((ROWS, FEATURES), BF16),
            shape((ROWS, HEAD), F32),
            shape((ROWS, GROUP * HEAD), F32),
            shape((ROWS, GROUP * HEAD), F32),
        ),
        in_specs=[hbm] * 7 + [pl.BlockSpec(memory_space=pltpu.SMEM)],
        out_specs=(vmem(),) * 4,
        scratch_shapes=[
            pltpu.VMEM((LENGTH, FEATURES), BF16),
            per_head,
            per_head,
            per_head,
            per_head,
            pltpu.VMEM((FEATURES, 3 * HEAD), BF16),
            table,
            table,
            scores,
            scores,
            table,
            table,
            pltpu.VMEM((HEAD, LENGTH), BF16),
            pltpu.VMEM((LENGTH, 3 * HEAD), BF16),
            blocks,
            blocks,
            blocks,
            pltpu.VMEM((RECV_ROWS, FEATURES), BF16),
            pieces,
            pieces,
            pieces,
            pieces,
            pltpu.VMEM((2, 8, 2, HEAD, ROWS), BF16),
            pair,
            pair,
            pltpu.VMEM((2, 8, HEAD, ROWS), BF16),
            dma((len(GATHER),)),
            dma((len(GATHER),)),
            dma((len(GATHER) + 1,)),
            dma((len(GATHER) + 1,)),
            dma((N_SEQ,)),
            dma((N_SEQ,)),
            dma((18,)),
            dma((18,)),
            dma((6,)),
            dma((len(REDUCE),)),
            dma((len(REDUCE),)),
            dma((len(ORDER),)),
            dma((len(ORDER),)),
            dma((4,)),
            dma((2, 8)),
            dma((2, 8)),
            dma((8,)),
            dma((8,)),
        ],
        compiler_params=pltpu.CompilerParams(collective_id=1, has_side_effects=True, vmem_limit_bytes=VMEM_LIMIT),
        name="attention_backward",
    )(x, g, wq, wk, wv, cos, sin, boundary)


def copy_kernel(*refs):
    for source, target in zip(refs[:4], refs[4:]):
        target[...] = source[...]


def place_outputs(*arrays):
    return pl.pallas_call(
        copy_kernel,
        out_shape=tuple(shape(a.shape, a.dtype) for a in arrays),
        in_specs=[vmem()] * 4,
        out_specs=(vmem(),) * 4,
        compiler_params=pltpu.CompilerParams(vmem_limit_bytes=VMEM_LIMIT),
        name="place_outputs",
    )(*arrays)


def shards(normed_input, out_grad, w_query, key_weight_matrix, value_weight_matrix, boundary):
    cos, sin = rope_tables()
    input_grad, dq, dk, dv = run(
        normed_input[0], out_grad[0], w_query, key_weight_matrix, value_weight_matrix,
        jnp.asarray(cos), jnp.asarray(sin), boundary,
    )
    input_grad, dq, dk, dv = place_outputs(input_grad, dq, dk, dv)
    return (input_grad[None], dq, dk, dv)


def solution(mesh):
    return jax.shard_map(
        shards,
        mesh=mesh,
        in_specs=(
            P("fsdp", "seq", None),
            P("fsdp", "seq", None),
            P("fsdp", "seq"),
            P("fsdp", None),
            P("fsdp", None),
            P("fsdp"),
        ),
        out_specs=(P("fsdp", "seq", None), P("fsdp", "seq"), P("fsdp", None), P("fsdp", None)),
        check_vma=False,
    )
```

```python
import jax
import jax.numpy as jnp
import numpy as np
from jax import lax
from jax.experimental import pallas as pl
from jax.experimental.pallas import tpu as pltpu
from jax.sharding import PartitionSpec as P

HEAD = 128
N_SEQ = 16
N_FSDP = 16
ROWS = 128
LENGTH = 2048
FEATURES = 2048
GROUP = 4
MESH = pl.DeviceIdType.MESH
SCALE = HEAD ** (-0.5)
EXP2_SCALE = SCALE * 1.4426950408889634

GATHER = (
    ("up", (0, 0), 0, 64, (-1, 0)),
    ("down", (0, 0), 64, 64, (1, 0)),
    ("side", (0, 0), 0, 64, (0, 1)),
    ("up", (0, 0), 64, 64, (-1, 0)),
    ("down", (0, 0), 0, 64, (1, 0)),
    ("side", (0, 0), 64, 64, (0, 1)),
    ("up", (-1, 0), 0, 64, (2, 0)),
    ("down", (1, 0), 64, 64, (2, 0)),
    ("side", (-1, 0), 0, 48, (-1, 1)),
    ("side", (1, 0), 80, 48, (1, 1)),
    ("down", (0, 1), 0, 64, (1, 1)),
    ("up", (0, 1), 64, 64, (-1, 1)),
    ("up", (-1, 1), 0, 48, (2, 1)),
    ("down", (1, 1), 80, 48, (2, 1)),
    ("side", (2, 0), 48, 32, (2, 1)),
    ("side", (-1, 0), 48, 16, (-1, 1)),
    ("side", (1, 0), 64, 16, (1, 1)),
)

REDUCE = (
    ("down", (2, 1), 0, 48, (-1, 1)),
    ("up", (2, 1), 80, 48, (1, 1)),
    ("side", (2, 1), 48, 32, (2, 0)),
    ("down", (-1, 1), 64, 64, (0, 1)),
    ("up", (1, 1), 0, 64, (0, 1)),
    ("side", (-1, 1), 48, 16, (-1, 0)),
    ("side", (1, 1), 64, 16, (1, 0)),
    ("side", (-1, 1), 0, 48, (-1, 0)),
    ("side", (1, 1), 80, 48, (1, 0)),
    ("down", (2, 0), 0, 64, (-1, 0)),
    ("up", (2, 0), 64, 64, (1, 0)),
    ("down", (-1, 0), 64, 64, (0, 0)),
    ("up", (1, 0), 0, 64, (0, 0)),
    ("side", (0, 1), 0, 64, (0, 0)),
    ("side", (0, 1), 64, 64, (0, 0)),
    ("down", (-1, 0), 0, 64, (0, 0)),
    ("up", (1, 0), 64, 64, (0, 0)),
)
LAST = ((0, (12, 13, 15)), (64, (11, 14, 16)))


class Place:
    def __init__(self):
        self.f = lax.axis_index("fsdp")
        self.s = lax.axis_index("seq")
        self.core = lax.rem(self.s, 2)
        self.hi = lax.rem(lax.div(self.s, 2), 2)
        self.y = lax.div(self.s, 4)
        self.z = lax.rem(self.f, 8)
        self.lo = lax.div(self.f, 8)

    def to(self, direction):
        s = self.s
        if direction == "up":
            return (self.f, lax.rem(s + 4, N_SEQ))
        if direction == "down":
            return (self.f, lax.rem(s + 12, N_SEQ))
        if direction == "side":
            return (self.f, s + 2 - 4 * self.hi)
        if direction == "lo":
            return ((1 - self.lo) * 8 + self.z, s)
        return (self.f, s + 1 - 2 * self.core)

    def block(self, rel, other_core=0):
        dy, dh = rel
        y = lax.rem(self.y + dy + 4, 4)
        hi = 1 - self.hi if dh else self.hi
        core = 1 - self.core if other_core else self.core
        return y * 4 + hi * 2 + core


def enter(me):
    barrier = pltpu.get_barrier_semaphore()

    def greet(device):
        pl.semaphore_signal(barrier, inc=1, device_id=device, device_id_type=MESH)

    def greet_seq(j, carry):
        greet((me.f, lax.rem(me.s + j, N_SEQ)))
        return carry

    def greet_z(j, carry):
        greet((me.lo * 8 + lax.rem(me.z + j, 8), me.s))
        return carry

    lax.fori_loop(1, N_SEQ, greet_seq, 0)
    lax.fori_loop(1, 8, greet_z, 0)
    greet(me.to("lo"))
    pl.semaphore_wait(barrier, N_SEQ - 1 + 8)


def remote(src, dst, send, recv, device):
    return pltpu.make_async_remote_copy(
        src_ref=src,
        dst_ref=dst,
        send_sem=send,
        recv_sem=recv,
        device_id=device,
        device_id_type=MESH,
    )


CHIP_PARTS = (
    ((-1, 0), (0, 3)),
    ((1, 0), (1, 4)),
    ((0, 1), (2, 5)),
    ((2, 0), (6, 7)),
    ((-1, 1), (8, 11, 15)),
    ((1, 1), (9, 10, 16)),
    ((2, 1), (12, 13, 14)),
)


def gather(
    me, x_hbm, g_hbm, wq_hbm, wk_hbm, wv_hbm, cos_hbm, sin_hbm,
    rows, q_ref, k_ref, v_ref, grad_ref, w_ref,
    cos_ref, sin_ref, x_send, x_recv, c_send, c_recv, g_send, g_recv, w_send, w_recv, l_sem,
):
    own = pl.multiple_of(me.s * ROWS, ROWS)
    head_col = pl.multiple_of(me.y * HEAD, HEAD)
    own_w = pl.ds(pl.multiple_of(me.f * ROWS, ROWS), ROWS)
    loads = [
        pltpu.make_async_copy(wq_hbm, w_ref.at[own_w, pl.ds(0, HEAD)], l_sem.at[0]),
        pltpu.make_async_copy(wk_hbm.at[:, pl.ds(head_col, HEAD)], w_ref.at[own_w, pl.ds(HEAD, HEAD)], l_sem.at[1]),
        pltpu.make_async_copy(wv_hbm.at[:, pl.ds(head_col, HEAD)], w_ref.at[own_w, pl.ds(HEAD, HEAD)], l_sem.at[1]),
        pltpu.make_async_copy(x_hbm, rows.at[pl.ds(own, ROWS), :], l_sem.at[2]),
        pltpu.make_async_copy(cos_hbm, cos_ref, l_sem.at[3]),
        pltpu.make_async_copy(sin_hbm, sin_ref, l_sem.at[4]),
        pltpu.make_async_copy(g_hbm.at[:, pl.ds(own, HEAD)], grad_ref.at[pl.ds(own, ROWS), :], l_sem.at[5]),
    ]
    loads[0].start()

    @pl.when(me.core == 0)
    def _():
        loads[1].start()

    @pl.when(me.core == 1)
    def _():
        loads[2].start()

    for load in loads[3:]:
        load.start()

    enter(me)

    def w_piece(lo, z):
        at = pl.multiple_of((lo * 8 + z) * ROWS, ROWS)
        return w_ref.at[pl.ds(at, ROWS), pl.ds(0, 2 * HEAD)]

    def w_copy(lo, z, slot, device):
        piece = w_piece(lo, z)
        return remote(piece, piece, w_send.at[slot], w_recv.at[slot], device)

    def along(dz):
        return (me.lo * 8 + lax.rem(me.z + dz + 8, 8), me.s)

    def w_move(other, held, hop):
        lo = 1 - me.lo if other else me.lo
        return w_copy(lo, lax.rem(me.z + held + 8, 8), 9 * other + 4 + hop - held, along(hop))

    def w_arrival(other, away):
        lo = 1 - me.lo if other else me.lo
        return w_copy(lo, lax.rem(me.z + away + 8, 8), 9 * other + 4 - away, along(1))

    first_moves = [(0, hop) for hop in (1, -1, 2, -2)]
    next_moves = {0: ((-2, 1), (2, -1), (-2, 2)), 1: ((-2, 1), (2, -1), (2, -2))}

    def w_start(other):
        for held, hop in first_moves:
            w_move(other, held, hop).start()

    def w_onward(other):
        w_arrival(other, -2).wait_recv()
        w_arrival(other, 2).wait_recv()
        for held, hop in next_moves[other]:
            w_move(other, held, hop).start()

    def w_finish():
        for other in (0, 1):
            for away in (-1, 1, -3, 3, -4 if other == 0 else 4):
                w_arrival(other, away).wait_recv()

    def w_sent():
        for other in (0, 1):
            for held, hop in first_moves + list(next_moves[other]):
                w_move(other, held, hop).wait_send()

    def part(rel, first, count, other_core=0):
        at = pl.multiple_of(me.block(rel, other_core) * ROWS + first, 16)
        return rows.at[pl.ds(at, count), :]

    def x_copy(i):
        direction, rel, first, count, _ = GATHER[i]
        piece = part(rel, first, count)
        source = x_hbm.at[pl.ds(first, count), :] if rel == (0, 0) else piece
        return remote(source, piece, x_send.at[i], x_recv.at[i], me.to(direction))

    def x_start(i):
        x_copy(i).start()

    def x_arrived(i):
        direction, _, first, count, rel = GATHER[i]
        piece = part(rel, first, count)
        remote(piece, piece, x_send.at[i], x_recv.at[i], me.to(direction)).wait_recv()
        core_copy(i).start()

    def core_copy(i, receive=False):
        rel, first, count = (0, 0), 0, 128
        if i < len(GATHER):
            _, _, first, count, rel = GATHER[i]
        piece = part(rel, first, count, other_core=1 if receive else 0)
        source = x_hbm if rel == (0, 0) and not receive else piece
        return remote(source, piece, c_send.at[i], c_recv.at[i], me.to("core"))

    def g_copy(j, device_s, source_s):
        at = pl.multiple_of(source_s * ROWS, ROWS)
        col = pl.multiple_of(device_s * HEAD, HEAD)
        return remote(
            g_hbm.at[:, pl.ds(col, HEAD)],
            grad_ref.at[pl.ds(at, ROWS), :],
            g_send.at[j],
            g_recv.at[j],
            (me.f, device_s),
        )

    def g_start(j, carry):
        g_copy(j, lax.rem(me.s + j, N_SEQ), me.s).start()
        return carry

    def project(rel, parts):
        for i in parts:
            core_copy(i, True).wait_recv()
        hi = 1 - me.hi if rel[1] else me.hi
        chip = lax.rem(me.y + rel[0] + 4, 4) * 2 + hi
        at = pl.ds(pl.multiple_of(chip * 256, 256), 256)
        full = jnp.dot(rows[at, :], w_ref[...], preferred_element_type=jnp.float32)
        cos, sin = cos_ref[at, :], sin_ref[at, :]
        q, first, second = full[:, :HEAD], full[:, HEAD : 2 * HEAD], full[:, 2 * HEAD :]
        is_key = me.core == 0
        k, v = jnp.where(is_key, first, second), jnp.where(is_key, second, first)
        q_ref[at, :] = (q * cos + pltpu.roll(q, HEAD // 2, 1) * sin).astype(jnp.bfloat16)
        k_ref[at, :] = (k * cos + pltpu.roll(k, HEAD // 2, 1) * sin).astype(jnp.bfloat16)
        v_ref[at, :] = v.astype(jnp.bfloat16)

    loads[0].wait()
    loads[1].wait()
    own_to_lo = w_copy(me.lo, me.z, 4, me.to("lo"))
    own_to_lo.start()
    for i in range(6):
        x_start(i)
    w_start(0)
    core_copy(len(GATHER)).start()
    w_copy(1 - me.lo, me.z, 4, me.to("lo")).wait_recv()
    w_start(1)
    x_arrived(0)
    x_start(6)
    x_start(8)
    x_arrived(1)
    x_start(7)
    x_start(9)
    x_start(15)
    x_start(16)
    x_arrived(2)
    x_start(10)
    x_arrived(5)
    x_start(11)
    w_onward(0)
    w_onward(1)
    x_arrived(3)
    x_arrived(4)
    x_arrived(8)
    x_start(12)
    x_arrived(9)
    x_start(13)
    x_arrived(6)
    x_arrived(7)
    x_start(14)
    lax.fori_loop(1, N_SEQ, g_start, 0)
    for load in loads[3:]:
        load.wait()
    w_finish()
    share = remote(
        w_ref.at[:, pl.ds(HEAD, HEAD)],
        w_ref.at[:, pl.ds(2 * HEAD, HEAD)],
        w_send.at[17],
        w_recv.at[17],
        me.to("core"),
    )
    share.start()
    x_arrived(10)
    x_arrived(11)
    x_arrived(15)
    x_arrived(16)
    share.wait_recv()
    project((0, 0), (len(GATHER),))
    for rel, parts in CHIP_PARTS[:4]:
        project(rel, parts)
    for rel, parts in CHIP_PARTS[4:6]:
        project(rel, parts)
    for i in CHIP_PARTS[6][1]:
        x_arrived(i)
    project(*CHIP_PARTS[6])

    def g_finish(j, carry):
        back = lax.rem(me.s + N_SEQ - j, N_SEQ)
        g_copy(j, back, back).wait_recv()
        g_copy(j, lax.rem(me.s + j, N_SEQ), me.s).wait_send()
        return carry

    lax.fori_loop(1, N_SEQ, g_finish, 0)
    share.wait_send()
    own_to_lo.wait_send()
    w_sent()
    for i in range(len(GATHER)):
        x_copy(i).wait_send()
    for i in range(len(GATHER) + 1):
        core_copy(i).wait_send()


NT = (((1,), (1,)), ((), ()))
TN = (((0,), (0,)), ((), ()))
QB = 512


def attention(me, b_ref, q_ref, k_ref, v_ref, g_ref, cos_ref, sin_ref, out_ref, sc, dp_sc, dk_sc, dv_sc, kt_sc):
    start = b_ref[0]
    kt_sc[...] = k_ref[...].T
    for i in range(LENGTH // QB):
        rows_i = pl.ds(i * QB, QB)
        q = q_ref[rows_i, :]
        g = g_ref[rows_i, :]
        q_pos = i * QB + lax.broadcasted_iota(jnp.int32, (1, QB), 1)
        low = jnp.where(q_pos < start, 0, start)
        top = jnp.full((1, QB), -1e30, jnp.float32)
        for j in range(i + 1):
            at = pl.ds(j * QB, QB)
            s = lax.dot_general(k_ref[at, :], q, NT, preferred_element_type=jnp.float32)
            k_pos = j * QB + lax.broadcasted_iota(jnp.int32, (QB, QB), 0)
            ok = k_pos >= low
            if j == i:
                ok = ok & (k_pos <= q_pos)
            s = jnp.where(ok, s, -1e30)
            sc[at, :] = s
            top = jnp.maximum(top, jnp.max(s, axis=0, keepdims=True))
        top = top * EXP2_SCALE
        total = jnp.zeros((1, QB), jnp.float32)
        for j in range(i + 1):
            at = pl.ds(j * QB, QB)
            e = jnp.exp2(sc[at, :] * EXP2_SCALE - top)
            sc[at, :] = e
            total = total + jnp.sum(e, axis=0, keepdims=True)
        inverse = 1.0 / total
        delta = jnp.zeros((1, QB), jnp.float32)
        for j in range(i + 1):
            at = pl.ds(j * QB, QB)
            p = sc[at, :] * inverse
            sc[at, :] = p
            low_p = p.astype(jnp.bfloat16)
            d = lax.dot_general(v_ref[at, :], g, NT, preferred_element_type=jnp.float32)
            dp_sc[at, :] = d
            delta = delta + jnp.sum(low_p.astype(jnp.float32) * d, axis=0, keepdims=True)
            dv = jnp.dot(low_p, g, preferred_element_type=jnp.float32)
            if j == i:
                dv_sc[at, :] = dv
            else:
                dv_sc[at, :] += dv
        dq = jnp.zeros((HEAD, QB), jnp.float32)
        for j in range(i + 1):
            at = pl.ds(j * QB, QB)
            ds = (sc[at, :] * (dp_sc[at, :] - delta)).astype(jnp.bfloat16)
            dk = jnp.dot(ds, q, preferred_element_type=jnp.float32)
            if j == i:
                dk_sc[at, :] = dk
            else:
                dk_sc[at, :] += dk
            dq = dq + jnp.dot(kt_sc[:, at], ds, preferred_element_type=jnp.float32)
        dq = dq.T * SCALE
        out_ref[rows_i, :HEAD] = (
            dq * cos_ref[rows_i, :] - pltpu.roll(dq, HEAD // 2, 1) * sin_ref[rows_i, :]
        ).astype(jnp.bfloat16)

    key_col = pl.ds(pl.multiple_of(HEAD + me.core * HEAD, HEAD), HEAD)
    value_col = pl.ds(pl.multiple_of(2 * HEAD - me.core * HEAD, HEAD), HEAD)

    def finish(c, carry):
        at = pl.ds(pl.multiple_of(c * QB, QB), QB)
        dk = dk_sc[at, :] * SCALE
        out_ref[at, key_col] = (
            dk * cos_ref[at, :] - pltpu.roll(dk, HEAD // 2, 1) * sin_ref[at, :]
        ).astype(jnp.bfloat16)
        out_ref[at, value_col] = dv_sc[at, :].astype(jnp.bfloat16)
        return carry

    lax.fori_loop(0, LENGTH // QB, finish, 0)


ORDER = ((2, 1), (-1, 1), (1, 1), (2, 0), (0, 1), (-1, 0), (1, 0), (0, 0))
SLOT = {rel: n for n, rel in enumerate(ORDER)}
RECV_AT = []
_at = 0
for _piece in REDUCE:
    RECV_AT.append(_at)
    _at += _piece[3]
RECV_ROWS = _at


def scatter(
    me, g_ref, w_ref, rows, in_ref, dq_ref, dk_ref, dv_ref,
    both, near, arrived, dwq, dwm, dwo, kv_near, f_in, lo_out, lo_in, kv_all,
    r_send, r_recv, n_send, n_recv, kv_sem, f_send, f_recv, a_send, a_recv,
):
    def near_copy(n):
        return remote(both.at[n, 1 - me.core], near.at[n], n_send.at[n], n_recv.at[n], me.to("core"))

    def block_out(rel):
        n = SLOT[rel]
        chip_rows = pl.ds(pl.multiple_of(lax.div(me.block(rel), 2) * 2 * ROWS, 2 * ROWS), 2 * ROWS)
        part = lax.dot_general(
            g_ref[chip_rows, :], w_ref[...], NT, preferred_element_type=jnp.float32
        ).astype(jnp.bfloat16)
        both[n, 0] = part[:ROWS]
        both[n, 1] = part[ROWS:]
        near_copy(n).start()

    def block_in(rel):
        n = SLOT[rel]
        near_copy(n).wait_recv()
        both[n, me.core] = (both[n, me.core].astype(jnp.float32) + near[n].astype(jnp.float32)).astype(
            jnp.bfloat16
        )

    def r_copy(i):
        direction, rel, first, count, _ = REDUCE[i]
        return remote(
            both.at[SLOT[rel], me.core, pl.ds(first, count), :],
            arrived.at[pl.ds(RECV_AT[i], count), :],
            r_send.at[i],
            r_recv.at[i],
            me.to(direction),
        )

    def r_add(i):
        _, _, first, count, rel = REDUCE[i]
        r_copy(i).wait_recv()
        n = SLOT[rel]
        both[n, me.core, pl.ds(first, count), :] = (
            both[n, me.core, pl.ds(first, count), :].astype(jnp.float32)
            + arrived[pl.ds(RECV_AT[i], count), :].astype(jnp.float32)
        ).astype(jnp.bfloat16)

    def weights(first_col, count, targets):
        def step(c, carry):
            at = pl.ds(pl.multiple_of(c * 512, 512), 512)
            part = lax.dot_general(
                g_ref[:, pl.ds(first_col, count)], rows[:, at], TN, preferred_element_type=jnp.float32
            ).astype(jnp.bfloat16)
            for n, target in enumerate(targets):
                for k in range(4):
                    target[lax.div(c, 2), lax.rem(c, 2) * 4 + k] = part[
                        n * HEAD : (n + 1) * HEAD, k * ROWS : (k + 1) * ROWS
                    ]
            return carry

        lax.fori_loop(0, FEATURES // 512, step, 0)

    kv_copy = remote(dwo, kv_near, kv_sem.at[0], kv_sem.at[1], me.to("core"))

    def f_copy(source, kind, j):
        to = lax.rem(me.z + j, 8)
        return remote(
            source.at[:, to], f_in.at[kind, j], f_send.at[kind, j], f_recv.at[kind, j], (me.lo * 8 + to, me.s)
        )

    def f_start(source, kind):
        def step(j, carry):
            f_copy(source, kind, j).start()
            return carry

        lax.fori_loop(1, 8, step, 0)

    def lo_copy(kind):
        return remote(lo_out.at[kind], lo_in.at[kind], f_send.at[kind, 0], f_recv.at[kind, 0], me.to("lo"))

    def f_sum(source, kind):
        def step(j, totals):
            f_copy(source, kind, j).wait()
            return (
                totals[0] + f_in[kind, j, me.lo].astype(jnp.float32),
                totals[1] + f_in[kind, j, 1 - me.lo].astype(jnp.float32),
            )

        own, other = lax.fori_loop(
            1,
            8,
            step,
            (source[me.lo, me.z].astype(jnp.float32), source[1 - me.lo, me.z].astype(jnp.float32)),
        )
        lo_out[kind] = other.astype(jnp.bfloat16)
        lo_copy(kind).start()
        return own

    def f_total(own, kind):
        lo_copy(kind).wait()
        return own + lo_in[kind].astype(jnp.float32)

    chip = lax.div(me.s, 2)

    def a_copy(j, source):
        slot = kv_all.at[me.core, source]
        to = (me.f, lax.rem(me.s + 2 * j, N_SEQ))
        return remote(slot, slot, a_send.at[j], a_recv.at[j], to)

    def a_start(j, carry):
        a_copy(j, chip).start()
        return carry

    def a_arrived(j, carry):
        a_copy(j, lax.rem(chip + 8 - j, 8)).wait_recv()
        return carry

    def a_sent(j, carry):
        a_copy(j, chip).wait_send()
        return carry

    def r_start(*pieces):
        for i in pieces:
            r_copy(i).start()

    block_out((2, 1))
    block_out((-1, 1))
    block_in((2, 1))
    r_start(0, 1, 2)
    block_out((1, 1))
    block_in((-1, 1))
    r_start(3, 5)
    block_in((1, 1))
    r_start(4, 6)
    weights(HEAD, 2 * HEAD, (dwm, dwo))
    kv_copy.start()
    block_out((2, 0))
    r_add(0)
    r_start(7)
    r_add(1)
    r_start(8)
    kv_copy.wait_recv()

    def kv_add(z, carry):
        for lo in (0, 1):
            dwm[lo, z] = (dwm[lo, z].astype(jnp.float32) + kv_near[lo, z].astype(jnp.float32)).astype(
                jnp.bfloat16
            )
        return carry

    lax.fori_loop(0, 8, kv_add, 0)
    f_start(dwm, 1)
    block_in((2, 0))
    r_add(2)
    r_start(9, 10)
    block_out((-1, 0))
    block_out((1, 0))
    block_in((-1, 0))
    r_start(11)
    block_in((1, 0))
    r_start(12)
    weights(0, HEAD, (dwq,))
    f_start(dwq, 0)
    block_out((0, 1))
    block_out((0, 0))
    block_in((0, 1))
    r_add(3)
    r_add(4)
    r_start(13, 14)
    block_in((0, 0))
    r_add(5)
    r_add(7)
    r_add(6)
    r_add(8)
    r_add(9)
    r_start(15)
    r_add(10)
    r_start(16)
    kv_own = f_sum(dwm, 1)
    kv_all[me.core, chip] = f_total(kv_own, 1).astype(jnp.bfloat16)
    lax.fori_loop(1, 8, a_start, 0)
    q_own = f_sum(dwq, 0)
    lax.fori_loop(1, 8, a_arrived, 0)
    kv_mine, kv_theirs = kv_all.at[me.core], kv_all.at[1 - me.core]
    kv_share = remote(kv_mine, kv_mine, kv_sem.at[2], kv_sem.at[3], me.to("core"))
    kv_share.start()
    for first, pieces in LAST:
        total = both[SLOT[(0, 0)], me.core, pl.ds(first, 64), :].astype(jnp.float32)
        for i in pieces:
            r_copy(i).wait_recv()
            total = total + arrived[pl.ds(RECV_AT[i], 64), :].astype(jnp.float32)
        in_ref[pl.ds(first, 64), :] = total.astype(jnp.bfloat16)
    dq_ref[...] = f_total(q_own, 0).T
    remote(kv_theirs, kv_theirs, kv_sem.at[2], kv_sem.at[3], me.to("core")).wait_recv()
    for n in range(4):
        at = pl.ds(n * HEAD, HEAD)
        for kind, out in ((0, dk_ref), (1, dv_ref)):
            out[:, at] = (
                kv_all[kind, 2 * n].astype(jnp.float32) + kv_all[kind, 2 * n + 1].astype(jnp.float32)
            ).T
    lax.fori_loop(1, 8, a_sent, 0)
    kv_share.wait_send()
    kv_copy.wait_send()
    for i in range(len(REDUCE)):
        r_copy(i).wait_send()
    for n in range(len(ORDER)):
        near_copy(n).wait_send()


def whole_kernel(
    x_hbm, g_hbm, wq_hbm, wk_hbm, wv_hbm, cos_hbm, sin_hbm, b_ref,
    in_ref, dq_ref, dk_ref, dv_ref,
    rows, q_ref, k_ref, v_ref, grad_ref, w_ref, cos_ref, sin_ref,
    sc, dp_sc, dk_sc, dv_sc, kt_sc, cols,
    both, near, arrived, dwq, dwm, dwo, kv_near, f_in, lo_out, lo_in, kv_all,
    *sems,
):
    me = Place()
    gather(
        me, x_hbm, g_hbm, wq_hbm, wk_hbm, wv_hbm, cos_hbm, sin_hbm,
        rows, q_ref, k_ref, v_ref, grad_ref, w_ref, cos_ref, sin_ref, *sems[:9],
    )
    attention(me, b_ref, q_ref, k_ref, v_ref, grad_ref, cos_ref, sin_ref, cols, sc, dp_sc, dk_sc, dv_sc, kt_sc)
    scatter(
        me, cols, w_ref, rows, in_ref, dq_ref, dk_ref, dv_ref,
        both, near, arrived, dwq, dwm, dwo, kv_near, f_in, lo_out, lo_in, kv_all, *sems[9:],
    )


def rope_tables():
    half = HEAD // 2
    inverse = (500000.0 ** (-(np.arange(half, dtype=np.float64) * 2.0 / HEAD))).astype(np.float32)
    angles = np.arange(LENGTH, dtype=np.float32)[:, None] * inverse[None, :]
    cos, sin = np.cos(angles), np.sin(angles)
    return np.concatenate([cos, cos], axis=1), np.concatenate([-sin, sin], axis=1)


def vmem():
    return pl.BlockSpec(memory_space=pltpu.VMEM)


BF16, F32 = jnp.bfloat16, jnp.float32
dma = pltpu.SemaphoreType.DMA
shape = jax.ShapeDtypeStruct
VMEM_LIMIT = 62 * 2**20


def run(x, g, wq, wk, wv, cos, sin, boundary):
    per_head = pltpu.VMEM((LENGTH, HEAD), BF16)
    table = pltpu.VMEM((LENGTH, HEAD), F32)
    scores = pltpu.VMEM((LENGTH, QB), F32)
    blocks = pltpu.VMEM((8, ROWS, FEATURES), BF16)
    pieces = pltpu.VMEM((2, 8, HEAD, ROWS), BF16)
    pair = pltpu.VMEM((2, HEAD, ROWS), BF16)
    hbm = pl.BlockSpec(memory_space=pltpu.HBM)
    return pl.pallas_call(
        whole_kernel,
        out_shape=(
            shape((ROWS, FEATURES), BF16),
            shape((ROWS, HEAD), F32),
            shape((ROWS, GROUP * HEAD), F32),
            shape((ROWS, GROUP * HEAD), F32),
        ),
        in_specs=[hbm] * 7 + [pl.BlockSpec(memory_space=pltpu.SMEM)],
        out_specs=(vmem(),) * 4,
        scratch_shapes=[
            pltpu.VMEM((LENGTH, FEATURES), BF16),
            per_head,
            per_head,
            per_head,
            per_head,
            pltpu.VMEM((FEATURES, 3 * HEAD), BF16),
            table,
            table,
            scores,
            scores,
            table,
            table,
            pltpu.VMEM((HEAD, LENGTH), BF16),
            pltpu.VMEM((LENGTH, 3 * HEAD), BF16),
            pltpu.VMEM((8, 2, ROWS, FEATURES), BF16),
            blocks,
            pltpu.VMEM((RECV_ROWS, FEATURES), BF16),
            pieces,
            pieces,
            pieces,
            pieces,
            pltpu.VMEM((2, 8, 2, HEAD, ROWS), BF16),
            pair,
            pair,
            pltpu.VMEM((2, 8, HEAD, ROWS), BF16),
            dma((len(GATHER),)),
            dma((len(GATHER),)),
            dma((len(GATHER) + 1,)),
            dma((len(GATHER) + 1,)),
            dma((N_SEQ,)),
            dma((N_SEQ,)),
            dma((18,)),
            dma((18,)),
            dma((6,)),
            dma((len(REDUCE),)),
            dma((len(REDUCE),)),
            dma((len(ORDER),)),
            dma((len(ORDER),)),
            dma((4,)),
            dma((2, 8)),
            dma((2, 8)),
            dma((8,)),
            dma((8,)),
        ],
        compiler_params=pltpu.CompilerParams(collective_id=1, has_side_effects=True, vmem_limit_bytes=VMEM_LIMIT),
        name="attention_backward",
    )(x, g, wq, wk, wv, cos, sin, boundary)


def copy_kernel(*refs):
    for source, target in zip(refs[:4], refs[4:]):
        target[...] = source[...]


def place_outputs(*arrays):
    return pl.pallas_call(
        copy_kernel,
        out_shape=tuple(shape(a.shape, a.dtype) for a in arrays),
        in_specs=[vmem()] * 4,
        out_specs=(vmem(),) * 4,
        compiler_params=pltpu.CompilerParams(vmem_limit_bytes=VMEM_LIMIT),
        name="place_outputs",
    )(*arrays)


def shards(normed_input, out_grad, w_query, key_weight_matrix, value_weight_matrix, boundary):
    cos, sin = rope_tables()
    input_grad, dq, dk, dv = run(
        normed_input[0], out_grad[0], w_query, key_weight_matrix, value_weight_matrix,
        jnp.asarray(cos), jnp.asarray(sin), boundary,
    )
    input_grad, dq, dk, dv = place_outputs(input_grad, dq, dk, dv)
    return (input_grad[None], dq, dk, dv)


def solution(mesh):
    return jax.shard_map(
        shards,
        mesh=mesh,
        in_specs=(
            P("fsdp", "seq", None),
            P("fsdp", "seq", None),
            P("fsdp", "seq"),
            P("fsdp", None),
            P("fsdp", None),
            P("fsdp"),
        ),
        out_specs=(P("fsdp", "seq", None), P("fsdp", "seq"), P("fsdp", None), P("fsdp", None)),
        check_vma=False,
    )
```

```python
import jax
import jax.numpy as jnp
import numpy as np
from jax import lax
from jax.experimental import pallas as pl
from jax.experimental.pallas import tpu as pltpu
from jax.sharding import PartitionSpec as P

HEAD = 128
N_SEQ = 16
N_FSDP = 16
ROWS = 128
LENGTH = 2048
FEATURES = 2048
GROUP = 4
MESH = pl.DeviceIdType.MESH
SCALE = HEAD ** (-0.5)
EXP2_SCALE = SCALE * 1.4426950408889634

GATHER = (
    ("up", (0, 0), 0, 64, (-1, 0)),
    ("down", (0, 0), 64, 64, (1, 0)),
    ("side", (0, 0), 0, 64, (0, 1)),
    ("up", (0, 0), 64, 64, (-1, 0)),
    ("down", (0, 0), 0, 64, (1, 0)),
    ("side", (0, 0), 64, 64, (0, 1)),
    ("up", (-1, 0), 0, 64, (2, 0)),
    ("down", (1, 0), 64, 64, (2, 0)),
    ("side", (-1, 0), 0, 48, (-1, 1)),
    ("side", (1, 0), 80, 48, (1, 1)),
    ("down", (0, 1), 0, 64, (1, 1)),
    ("up", (0, 1), 64, 64, (-1, 1)),
    ("up", (-1, 1), 0, 48, (2, 1)),
    ("down", (1, 1), 80, 48, (2, 1)),
    ("side", (2, 0), 48, 32, (2, 1)),
    ("side", (-1, 0), 48, 16, (-1, 1)),
    ("side", (1, 0), 64, 16, (1, 1)),
)

REDUCE = (
    ("down", (2, 1), 0, 48, (-1, 1)),
    ("up", (2, 1), 80, 48, (1, 1)),
    ("side", (2, 1), 48, 32, (2, 0)),
    ("down", (-1, 1), 64, 64, (0, 1)),
    ("up", (1, 1), 0, 64, (0, 1)),
    ("side", (-1, 1), 48, 16, (-1, 0)),
    ("side", (1, 1), 64, 16, (1, 0)),
    ("side", (-1, 1), 0, 48, (-1, 0)),
    ("side", (1, 1), 80, 48, (1, 0)),
    ("down", (2, 0), 0, 64, (-1, 0)),
    ("up", (2, 0), 64, 64, (1, 0)),
    ("down", (-1, 0), 64, 64, (0, 0)),
    ("up", (1, 0), 0, 64, (0, 0)),
    ("side", (0, 1), 0, 64, (0, 0)),
    ("side", (0, 1), 64, 64, (0, 0)),
    ("down", (-1, 0), 0, 64, (0, 0)),
    ("up", (1, 0), 64, 64, (0, 0)),
)
LAST = ((0, (12, 13, 15)), (64, (11, 14, 16)))


class Place:
    def __init__(self):
        self.f = lax.axis_index("fsdp")
        self.s = lax.axis_index("seq")
        self.core = lax.rem(self.s, 2)
        self.hi = lax.rem(lax.div(self.s, 2), 2)
        self.y = lax.div(self.s, 4)
        self.z = lax.rem(self.f, 8)
        self.lo = lax.div(self.f, 8)

    def to(self, direction):
        s = self.s
        if direction == "up":
            return (self.f, lax.rem(s + 4, N_SEQ))
        if direction == "down":
            return (self.f, lax.rem(s + 12, N_SEQ))
        if direction == "side":
            return (self.f, s + 2 - 4 * self.hi)
        if direction == "lo":
            return ((1 - self.lo) * 8 + self.z, s)
        return (self.f, s + 1 - 2 * self.core)

    def block(self, rel, other_core=0):
        dy, dh = rel
        y = lax.rem(self.y + dy + 4, 4)
        hi = 1 - self.hi if dh else self.hi
        core = 1 - self.core if other_core else self.core
        return y * 4 + hi * 2 + core


def enter(me):
    barrier = pltpu.get_barrier_semaphore()

    def greet(device):
        pl.semaphore_signal(barrier, inc=1, device_id=device, device_id_type=MESH)

    def greet_seq(j, carry):
        greet((me.f, lax.rem(me.s + j, N_SEQ)))
        return carry

    def greet_z(j, carry):
        greet((me.lo * 8 + lax.rem(me.z + j, 8), me.s))
        return carry

    lax.fori_loop(1, N_SEQ, greet_seq, 0)
    lax.fori_loop(1, 8, greet_z, 0)
    greet(me.to("lo"))
    return barrier


def remote(src, dst, send, recv, device):
    return pltpu.make_async_remote_copy(
        src_ref=src,
        dst_ref=dst,
        send_sem=send,
        recv_sem=recv,
        device_id=device,
        device_id_type=MESH,
    )


CHIP_PARTS = (
    ((-1, 0), (0, 3)),
    ((1, 0), (1, 4)),
    ((0, 1), (2, 5)),
    ((2, 0), (6, 7)),
    ((-1, 1), (8, 11, 15)),
    ((1, 1), (9, 10, 16)),
    ((2, 1), (12, 13, 14)),
)


def gather(
    me, x_hbm, g_hbm, wq_hbm, wk_hbm, wv_hbm, cos_hbm, sin_hbm,
    rows, q_ref, k_ref, v_ref, grad_ref, w_ref,
    cos_ref, sin_ref, x_send, x_recv, c_send, c_recv, g_send, g_recv, w_send, w_recv, l_sem,
):
    barrier = enter(me)
    own = pl.multiple_of(me.s * ROWS, ROWS)
    head_col = pl.multiple_of(me.y * HEAD, HEAD)
    own_w = pl.ds(pl.multiple_of(me.f * ROWS, ROWS), ROWS)
    loads = [
        pltpu.make_async_copy(wq_hbm, w_ref.at[own_w, pl.ds(0, HEAD)], l_sem.at[0]),
        pltpu.make_async_copy(wk_hbm.at[:, pl.ds(head_col, HEAD)], w_ref.at[own_w, pl.ds(HEAD, HEAD)], l_sem.at[1]),
        pltpu.make_async_copy(wv_hbm.at[:, pl.ds(head_col, HEAD)], w_ref.at[own_w, pl.ds(HEAD, HEAD)], l_sem.at[1]),
        pltpu.make_async_copy(x_hbm, rows.at[pl.ds(own, ROWS), :], l_sem.at[2]),
        pltpu.make_async_copy(cos_hbm, cos_ref, l_sem.at[3]),
        pltpu.make_async_copy(sin_hbm, sin_ref, l_sem.at[4]),
        pltpu.make_async_copy(g_hbm.at[:, pl.ds(own, HEAD)], grad_ref.at[pl.ds(own, ROWS), :], l_sem.at[5]),
    ]
    loads[0].start()

    @pl.when(me.core == 0)
    def _():
        loads[1].start()

    @pl.when(me.core == 1)
    def _():
        loads[2].start()

    for load in loads[3:]:
        load.start()

    pl.semaphore_wait(barrier, N_SEQ - 1 + 8)

    def w_piece(lo, z):
        at = pl.multiple_of((lo * 8 + z) * ROWS, ROWS)
        return w_ref.at[pl.ds(at, ROWS), pl.ds(0, 2 * HEAD)]

    def w_copy(lo, z, slot, device):
        piece = w_piece(lo, z)
        return remote(piece, piece, w_send.at[slot], w_recv.at[slot], device)

    def along(dz):
        return (me.lo * 8 + lax.rem(me.z + dz + 8, 8), me.s)

    def w_move(other, held, hop):
        lo = 1 - me.lo if other else me.lo
        return w_copy(lo, lax.rem(me.z + held + 8, 8), 9 * other + 4 + hop - held, along(hop))

    def w_arrival(other, away):
        lo = 1 - me.lo if other else me.lo
        return w_copy(lo, lax.rem(me.z + away + 8, 8), 9 * other + 4 - away, along(1))

    first_moves = [(0, hop) for hop in (1, -1, 2, -2)]
    next_moves = {0: ((-2, 1), (2, -1), (-2, 2)), 1: ((-2, 1), (2, -1), (2, -2))}

    def w_start(other):
        for held, hop in first_moves:
            w_move(other, held, hop).start()

    def w_onward(other):
        w_arrival(other, -2).wait_recv()
        w_arrival(other, 2).wait_recv()
        for held, hop in next_moves[other]:
            w_move(other, held, hop).start()

    def w_finish():
        for other in (0, 1):
            for away in (-1, 1, -3, 3, -4 if other == 0 else 4):
                w_arrival(other, away).wait_recv()

    def w_sent():
        for other in (0, 1):
            for held, hop in first_moves + list(next_moves[other]):
                w_move(other, held, hop).wait_send()

    def part(rel, first, count, other_core=0):
        at = pl.multiple_of(me.block(rel, other_core) * ROWS + first, 16)
        return rows.at[pl.ds(at, count), :]

    def x_copy(i):
        direction, rel, first, count, _ = GATHER[i]
        piece = part(rel, first, count)
        source = x_hbm.at[pl.ds(first, count), :] if rel == (0, 0) else piece
        return remote(source, piece, x_send.at[i], x_recv.at[i], me.to(direction))

    def x_start(i):
        x_copy(i).start()

    def x_arrived(i):
        direction, _, first, count, rel = GATHER[i]
        piece = part(rel, first, count)
        remote(piece, piece, x_send.at[i], x_recv.at[i], me.to(direction)).wait_recv()
        core_copy(i).start()

    def core_copy(i, receive=False):
        rel, first, count = (0, 0), 0, 128
        if i < len(GATHER):
            _, _, first, count, rel = GATHER[i]
        piece = part(rel, first, count, other_core=1 if receive else 0)
        source = x_hbm if rel == (0, 0) and not receive else piece
        return remote(source, piece, c_send.at[i], c_recv.at[i], me.to("core"))

    def g_copy(j, device_s, source_s):
        at = pl.multiple_of(source_s * ROWS, ROWS)
        col = pl.multiple_of(device_s * HEAD, HEAD)
        return remote(
            g_hbm.at[:, pl.ds(col, HEAD)],
            grad_ref.at[pl.ds(at, ROWS), :],
            g_send.at[j],
            g_recv.at[j],
            (me.f, device_s),
        )

    def g_start(j, carry):
        g_copy(j, lax.rem(me.s + j, N_SEQ), me.s).start()
        return carry

    def project(rel, parts):
        for i in parts:
            core_copy(i, True).wait_recv()
        hi = 1 - me.hi if rel[1] else me.hi
        chip = lax.rem(me.y + rel[0] + 4, 4) * 2 + hi
        at = pl.ds(pl.multiple_of(chip * 256, 256), 256)
        full = jnp.dot(rows[at, :], w_ref[...], preferred_element_type=jnp.float32)
        cos, sin = cos_ref[at, :], sin_ref[at, :]
        q, first, second = full[:, :HEAD], full[:, HEAD : 2 * HEAD], full[:, 2 * HEAD :]
        is_key = me.core == 0
        k, v = jnp.where(is_key, first, second), jnp.where(is_key, second, first)
        q_ref[at, :] = (q * cos + pltpu.roll(q, HEAD // 2, 1) * sin).astype(jnp.bfloat16)
        k_ref[at, :] = (k * cos + pltpu.roll(k, HEAD // 2, 1) * sin).astype(jnp.bfloat16)
        v_ref[at, :] = v.astype(jnp.bfloat16)

    loads[0].wait()
    loads[1].wait()
    own_to_lo = w_copy(me.lo, me.z, 4, me.to("lo"))
    own_to_lo.start()
    for i in range(6):
        x_start(i)
    w_start(0)
    core_copy(len(GATHER)).start()
    w_copy(1 - me.lo, me.z, 4, me.to("lo")).wait_recv()
    w_start(1)
    x_arrived(0)
    x_start(6)
    x_start(8)
    x_arrived(1)
    x_start(7)
    x_start(9)
    x_start(15)
    x_start(16)
    x_arrived(2)
    x_start(10)
    x_arrived(5)
    x_start(11)
    w_onward(0)
    w_onward(1)
    x_arrived(3)
    x_arrived(4)
    x_arrived(8)
    x_start(12)
    x_arrived(9)
    x_start(13)
    x_arrived(6)
    x_arrived(7)
    x_start(14)
    lax.fori_loop(1, N_SEQ, g_start, 0)
    for load in loads[3:]:
        load.wait()
    w_finish()
    share = remote(
        w_ref.at[:, pl.ds(HEAD, HEAD)],
        w_ref.at[:, pl.ds(2 * HEAD, HEAD)],
        w_send.at[17],
        w_recv.at[17],
        me.to("core"),
    )
    share.start()
    x_arrived(10)
    x_arrived(11)
    x_arrived(15)
    x_arrived(16)
    share.wait_recv()
    project((0, 0), (len(GATHER),))
    for rel, parts in CHIP_PARTS[:4]:
        project(rel, parts)
    for rel, parts in CHIP_PARTS[4:6]:
        project(rel, parts)
    for i in CHIP_PARTS[6][1]:
        x_arrived(i)
    project(*CHIP_PARTS[6])

    def g_finish(j, carry):
        back = lax.rem(me.s + N_SEQ - j, N_SEQ)
        g_copy(j, back, back).wait_recv()
        g_copy(j, lax.rem(me.s + j, N_SEQ), me.s).wait_send()
        return carry

    lax.fori_loop(1, N_SEQ, g_finish, 0)
    share.wait_send()
    own_to_lo.wait_send()
    w_sent()
    for i in range(len(GATHER)):
        x_copy(i).wait_send()
    for i in range(len(GATHER) + 1):
        core_copy(i).wait_send()


NT = (((1,), (1,)), ((), ()))
TN = (((0,), (0,)), ((), ()))
QB = 512


def attention(me, b_ref, q_ref, k_ref, v_ref, g_ref, cos_ref, sin_ref, out_ref, sc, dp_sc, dk_sc, dv_sc, kt_sc):
    start = b_ref[0]
    kt_sc[...] = k_ref[...].T
    for i in range(LENGTH // QB):
        rows_i = pl.ds(i * QB, QB)
        q = q_ref[rows_i, :]
        g = g_ref[rows_i, :]
        q_pos = i * QB + lax.broadcasted_iota(jnp.int32, (1, QB), 1)
        low = jnp.where(q_pos < start, 0, start)
        top = jnp.full((1, QB), -1e30, jnp.float32)
        for j in range(i + 1):
            at = pl.ds(j * QB, QB)
            s = lax.dot_general(k_ref[at, :], q, NT, preferred_element_type=jnp.float32)
            k_pos = j * QB + lax.broadcasted_iota(jnp.int32, (QB, QB), 0)
            ok = k_pos >= low
            if j == i:
                ok = ok & (k_pos <= q_pos)
            s = jnp.where(ok, s, -1e30)
            sc[at, :] = s
            top = jnp.maximum(top, jnp.max(s, axis=0, keepdims=True))
        top = top * EXP2_SCALE
        total = jnp.zeros((1, QB), jnp.float32)
        for j in range(i + 1):
            at = pl.ds(j * QB, QB)
            e = jnp.exp2(sc[at, :] * EXP2_SCALE - top)
            sc[at, :] = e
            total = total + jnp.sum(e, axis=0, keepdims=True)
        inverse = 1.0 / total
        delta = jnp.zeros((1, QB), jnp.float32)
        for j in range(i + 1):
            at = pl.ds(j * QB, QB)
            p = sc[at, :] * inverse
            low_p = p.astype(jnp.bfloat16)
            d = lax.dot_general(v_ref[at, :], g, NT, preferred_element_type=jnp.float32)
            dp_sc[at, :] = d
            delta = delta + jnp.sum(low_p.astype(jnp.float32) * d, axis=0, keepdims=True)
            dv = jnp.dot(low_p, g, preferred_element_type=jnp.float32)
            if j == i:
                dv_sc[at, :] = dv
            else:
                dv_sc[at, :] += dv
        dq = jnp.zeros((HEAD, QB), jnp.float32)
        for j in range(i + 1):
            at = pl.ds(j * QB, QB)
            ds = (sc[at, :] * inverse * (dp_sc[at, :] - delta)).astype(jnp.bfloat16)
            dk = jnp.dot(ds, q, preferred_element_type=jnp.float32)
            if j == i:
                dk_sc[at, :] = dk
            else:
                dk_sc[at, :] += dk
            dq = dq + jnp.dot(kt_sc[:, at], ds, preferred_element_type=jnp.float32)
        dq = dq.T * SCALE
        out_ref[rows_i, :HEAD] = (
            dq * cos_ref[rows_i, :] - pltpu.roll(dq, HEAD // 2, 1) * sin_ref[rows_i, :]
        ).astype(jnp.bfloat16)

    key_col = pl.ds(pl.multiple_of(HEAD + me.core * HEAD, HEAD), HEAD)
    value_col = pl.ds(pl.multiple_of(2 * HEAD - me.core * HEAD, HEAD), HEAD)

    def finish(c, carry):
        at = pl.ds(pl.multiple_of(c * QB, QB), QB)
        dk = dk_sc[at, :] * SCALE
        out_ref[at, key_col] = (
            dk * cos_ref[at, :] - pltpu.roll(dk, HEAD // 2, 1) * sin_ref[at, :]
        ).astype(jnp.bfloat16)
        out_ref[at, value_col] = dv_sc[at, :].astype(jnp.bfloat16)
        return carry

    lax.fori_loop(0, LENGTH // QB, finish, 0)


ORDER = ((2, 1), (-1, 1), (1, 1), (2, 0), (0, 1), (-1, 0), (1, 0), (0, 0))
SLOT = {rel: n for n, rel in enumerate(ORDER)}
RECV_AT = []
_at = 0
for _piece in REDUCE:
    RECV_AT.append(_at)
    _at += _piece[3]
RECV_ROWS = _at


def scatter(
    me, g_ref, w_ref, rows, in_ref, dq_ref, dk_ref, dv_ref,
    both, near, arrived, dwq, dwm, dwo, kv_near, f_in, lo_out, lo_in, kv_all,
    r_send, r_recv, n_send, n_recv, kv_sem, f_send, f_recv, a_send, a_recv,
):
    def near_copy(n):
        return remote(both.at[n, 1 - me.core], near.at[n], n_send.at[n], n_recv.at[n], me.to("core"))

    def block_out(rel):
        n = SLOT[rel]
        chip_rows = pl.ds(pl.multiple_of(lax.div(me.block(rel), 2) * 2 * ROWS, 2 * ROWS), 2 * ROWS)
        part = lax.dot_general(
            g_ref[chip_rows, :], w_ref[...], NT, preferred_element_type=jnp.float32
        ).astype(jnp.bfloat16)
        both[n, 0] = part[:ROWS]
        both[n, 1] = part[ROWS:]
        near_copy(n).start()

    def block_in(rel):
        n = SLOT[rel]
        near_copy(n).wait_recv()
        both[n, me.core] = (both[n, me.core].astype(jnp.float32) + near[n].astype(jnp.float32)).astype(
            jnp.bfloat16
        )

    def r_copy(i):
        direction, rel, first, count, _ = REDUCE[i]
        return remote(
            both.at[SLOT[rel], me.core, pl.ds(first, count), :],
            arrived.at[pl.ds(RECV_AT[i], count), :],
            r_send.at[i],
            r_recv.at[i],
            me.to(direction),
        )

    def r_add(i):
        _, _, first, count, rel = REDUCE[i]
        r_copy(i).wait_recv()
        n = SLOT[rel]
        both[n, me.core, pl.ds(first, count), :] = (
            both[n, me.core, pl.ds(first, count), :].astype(jnp.float32)
            + arrived[pl.ds(RECV_AT[i], count), :].astype(jnp.float32)
        ).astype(jnp.bfloat16)

    def weights(first_col, count, targets):
        def step(c, carry):
            at = pl.ds(pl.multiple_of(c * 512, 512), 512)
            part = lax.dot_general(
                g_ref[:, pl.ds(first_col, count)], rows[:, at], TN, preferred_element_type=jnp.float32
            ).astype(jnp.bfloat16)
            for n, target in enumerate(targets):
                for k in range(4):
                    target[lax.div(c, 2), lax.rem(c, 2) * 4 + k] = part[
                        n * HEAD : (n + 1) * HEAD, k * ROWS : (k + 1) * ROWS
                    ]
            return carry

        lax.fori_loop(0, FEATURES // 512, step, 0)

    kv_copy = remote(dwo, kv_near, kv_sem.at[0], kv_sem.at[1], me.to("core"))

    def f_copy(source, kind, j):
        to = lax.rem(me.z + j, 8)
        return remote(
            source.at[:, to], f_in.at[kind, j], f_send.at[kind, j], f_recv.at[kind, j], (me.lo * 8 + to, me.s)
        )

    def f_start(source, kind):
        def step(j, carry):
            f_copy(source, kind, j).start()
            return carry

        lax.fori_loop(1, 8, step, 0)

    def lo_copy(kind):
        return remote(lo_out.at[kind], lo_in.at[kind], f_send.at[kind, 0], f_recv.at[kind, 0], me.to("lo"))

    def f_sum(source, kind):
        def step(j, totals):
            f_copy(source, kind, j).wait()
            return (
                totals[0] + f_in[kind, j, me.lo].astype(jnp.float32),
                totals[1] + f_in[kind, j, 1 - me.lo].astype(jnp.float32),
            )

        own, other = lax.fori_loop(
            1,
            8,
            step,
            (source[me.lo, me.z].astype(jnp.float32), source[1 - me.lo, me.z].astype(jnp.float32)),
        )
        lo_out[kind] = other.astype(jnp.bfloat16)
        lo_copy(kind).start()
        return own

    def f_total(own, kind):
        lo_copy(kind).wait()
        return own + lo_in[kind].astype(jnp.float32)

    chip = lax.div(me.s, 2)

    def a_copy(j, source):
        slot = kv_all.at[me.core, source]
        to = (me.f, lax.rem(me.s + 2 * j, N_SEQ))
        return remote(slot, slot, a_send.at[j], a_recv.at[j], to)

    def a_start(j, carry):
        a_copy(j, chip).start()
        return carry

    def a_arrived(j, carry):
        a_copy(j, lax.rem(chip + 8 - j, 8)).wait_recv()
        return carry

    def a_sent(j, carry):
        a_copy(j, chip).wait_send()
        return carry

    def r_start(*pieces):
        for i in pieces:
            r_copy(i).start()

    block_out((2, 1))
    block_out((-1, 1))
    block_in((2, 1))
    r_start(0, 1, 2)
    block_out((1, 1))
    block_in((-1, 1))
    r_start(3, 5)
    block_in((1, 1))
    r_start(4, 6)
    weights(HEAD, 2 * HEAD, (dwm, dwo))
    kv_copy.start()
    block_out((2, 0))
    r_add(0)
    r_start(7)
    r_add(1)
    r_start(8)
    kv_copy.wait_recv()

    def kv_add(z, carry):
        for lo in (0, 1):
            dwm[lo, z] = (dwm[lo, z].astype(jnp.float32) + kv_near[lo, z].astype(jnp.float32)).astype(
                jnp.bfloat16
            )
        return carry

    lax.fori_loop(0, 8, kv_add, 0)
    f_start(dwm, 1)
    block_in((2, 0))
    r_add(2)
    r_start(9, 10)
    block_out((-1, 0))
    block_out((1, 0))
    block_in((-1, 0))
    r_start(11)
    block_in((1, 0))
    r_start(12)
    block_out((0, 1))
    weights(0, HEAD, (dwq,))
    f_start(dwq, 0)
    block_out((0, 0))
    block_in((0, 1))
    r_add(3)
    r_add(4)
    r_start(13, 14)
    block_in((0, 0))
    r_add(5)
    r_add(7)
    r_add(6)
    r_add(8)
    r_add(9)
    r_start(15)
    r_add(10)
    r_start(16)
    kv_own = f_sum(dwm, 1)
    kv_all[me.core, chip] = f_total(kv_own, 1).astype(jnp.bfloat16)
    lax.fori_loop(1, 8, a_start, 0)
    q_own = f_sum(dwq, 0)
    lax.fori_loop(1, 8, a_arrived, 0)
    kv_mine, kv_theirs = kv_all.at[me.core], kv_all.at[1 - me.core]
    kv_share = remote(kv_mine, kv_mine, kv_sem.at[2], kv_sem.at[3], me.to("core"))
    kv_share.start()
    for first, pieces in LAST:
        total = both[SLOT[(0, 0)], me.core, pl.ds(first, 64), :].astype(jnp.float32)
        for i in pieces:
            r_copy(i).wait_recv()
            total = total + arrived[pl.ds(RECV_AT[i], 64), :].astype(jnp.float32)
        in_ref[pl.ds(first, 64), :] = total.astype(jnp.bfloat16)
    dq_ref[...] = f_total(q_own, 0).T
    remote(kv_theirs, kv_theirs, kv_sem.at[2], kv_sem.at[3], me.to("core")).wait_recv()
    for n in range(4):
        at = pl.ds(n * HEAD, HEAD)
        for kind, out in ((0, dk_ref), (1, dv_ref)):
            out[:, at] = (
                kv_all[kind, 2 * n].astype(jnp.float32) + kv_all[kind, 2 * n + 1].astype(jnp.float32)
            ).T
    lax.fori_loop(1, 8, a_sent, 0)
    kv_share.wait_send()
    kv_copy.wait_send()
    for i in range(len(REDUCE)):
        r_copy(i).wait_send()
    for n in range(len(ORDER)):
        near_copy(n).wait_send()


def whole_kernel(
    x_hbm, g_hbm, wq_hbm, wk_hbm, wv_hbm, cos_hbm, sin_hbm, b_ref,
    in_ref, dq_ref, dk_ref, dv_ref,
    rows, q_ref, k_ref, v_ref, grad_ref, w_ref, cos_ref, sin_ref,
    sc, dp_sc, dk_sc, dv_sc, kt_sc, cols,
    both, near, arrived, dwq, dwm, dwo, kv_near, f_in, lo_out, lo_in, kv_all,
    *sems,
):
    me = Place()
    gather(
        me, x_hbm, g_hbm, wq_hbm, wk_hbm, wv_hbm, cos_hbm, sin_hbm,
        rows, q_ref, k_ref, v_ref, grad_ref, w_ref, cos_ref, sin_ref, *sems[:9],
    )
    attention(me, b_ref, q_ref, k_ref, v_ref, grad_ref, cos_ref, sin_ref, cols, sc, dp_sc, dk_sc, dv_sc, kt_sc)
    scatter(
        me, cols, w_ref, rows, in_ref, dq_ref, dk_ref, dv_ref,
        both, near, arrived, dwq, dwm, dwo, kv_near, f_in, lo_out, lo_in, kv_all, *sems[9:],
    )


def rope_tables():
    half = HEAD // 2
    inverse = (500000.0 ** (-(np.arange(half, dtype=np.float64) * 2.0 / HEAD))).astype(np.float32)
    angles = np.arange(LENGTH, dtype=np.float32)[:, None] * inverse[None, :]
    cos, sin = np.cos(angles), np.sin(angles)
    return np.concatenate([cos, cos], axis=1), np.concatenate([-sin, sin], axis=1)


def vmem():
    return pl.BlockSpec(memory_space=pltpu.VMEM)


BF16, F32 = jnp.bfloat16, jnp.float32
dma = pltpu.SemaphoreType.DMA
shape = jax.ShapeDtypeStruct
VMEM_LIMIT = 62 * 2**20


def run(x, g, wq, wk, wv, cos, sin, boundary):
    per_head = pltpu.VMEM((LENGTH, HEAD), BF16)
    table = pltpu.VMEM((LENGTH, HEAD), F32)
    scores = pltpu.VMEM((LENGTH, QB), F32)
    blocks = pltpu.VMEM((8, ROWS, FEATURES), BF16)
    pieces = pltpu.VMEM((2, 8, HEAD, ROWS), BF16)
    pair = pltpu.VMEM((2, HEAD, ROWS), BF16)
    hbm = pl.BlockSpec(memory_space=pltpu.HBM)
    return pl.pallas_call(
        whole_kernel,
        out_shape=(
            shape((ROWS, FEATURES), BF16),
            shape((ROWS, HEAD), F32),
            shape((ROWS, GROUP * HEAD), F32),
            shape((ROWS, GROUP * HEAD), F32),
        ),
        in_specs=[hbm] * 7 + [pl.BlockSpec(memory_space=pltpu.SMEM)],
        out_specs=(vmem(),) * 4,
        scratch_shapes=[
            pltpu.VMEM((LENGTH, FEATURES), BF16),
            per_head,
            per_head,
            per_head,
            per_head,
            pltpu.VMEM((FEATURES, 3 * HEAD), BF16),
            table,
            table,
            scores,
            scores,
            table,
            table,
            pltpu.VMEM((HEAD, LENGTH), BF16),
            pltpu.VMEM((LENGTH, 3 * HEAD), BF16),
            pltpu.VMEM((8, 2, ROWS, FEATURES), BF16),
            blocks,
            pltpu.VMEM((RECV_ROWS, FEATURES), BF16),
            pieces,
            pieces,
            pieces,
            pieces,
            pltpu.VMEM((2, 8, 2, HEAD, ROWS), BF16),
            pair,
            pair,
            pltpu.VMEM((2, 8, HEAD, ROWS), BF16),
            dma((len(GATHER),)),
            dma((len(GATHER),)),
            dma((len(GATHER) + 1,)),
            dma((len(GATHER) + 1,)),
            dma((N_SEQ,)),
            dma((N_SEQ,)),
            dma((18,)),
            dma((18,)),
            dma((6,)),
            dma((len(REDUCE),)),
            dma((len(REDUCE),)),
            dma((len(ORDER),)),
            dma((len(ORDER),)),
            dma((4,)),
            dma((2, 8)),
            dma((2, 8)),
            dma((8,)),
            dma((8,)),
        ],
        compiler_params=pltpu.CompilerParams(collective_id=1, has_side_effects=True, vmem_limit_bytes=VMEM_LIMIT),
        name="attention_backward",
    )(x, g, wq, wk, wv, cos, sin, boundary)


def copy_kernel(*refs):
    for source, target in zip(refs[:4], refs[4:]):
        target[...] = source[...]


def place_outputs(*arrays):
    return pl.pallas_call(
        copy_kernel,
        out_shape=tuple(shape(a.shape, a.dtype) for a in arrays),
        in_specs=[vmem()] * 4,
        out_specs=(vmem(),) * 4,
        compiler_params=pltpu.CompilerParams(vmem_limit_bytes=VMEM_LIMIT),
        name="place_outputs",
    )(*arrays)


def shards(normed_input, out_grad, w_query, key_weight_matrix, value_weight_matrix, boundary):
    cos, sin = rope_tables()
    input_grad, dq, dk, dv = run(
        normed_input[0], out_grad[0], w_query, key_weight_matrix, value_weight_matrix,
        jnp.asarray(cos), jnp.asarray(sin), boundary,
    )
    input_grad, dq, dk, dv = place_outputs(input_grad, dq, dk, dv)
    return (input_grad[None], dq, dk, dv)


def solution(mesh):
    return jax.shard_map(
        shards,
        mesh=mesh,
        in_specs=(
            P("fsdp", "seq", None),
            P("fsdp", "seq", None),
            P("fsdp", "seq"),
            P("fsdp", None),
            P("fsdp", None),
            P("fsdp"),
        ),
        out_specs=(P("fsdp", "seq", None), P("fsdp", "seq"), P("fsdp", None), P("fsdp", None)),
        check_vma=False,
    )
```
